32 devices in a mesh: gx: 4 (over z), gy: 8 (over y, x, core).
Axes of the slice: x: 2, y: 2, z: 4, core: 2. Of those that a mesh axis runs over, the one named last changes fastest.
Arguments:
- movie: bfloat16 [32, 64, 128, 128], P('gx', 'gy'), may hold values from -14 to 14
- brain_mask: int32 [32, 64, 128], P('gx', 'gy'), may hold values 0 or 1
Outputs:
- fitted: bfloat16 [32, 64, 128, 128], P('gx', 'gy')
- propagator: float32 [127, 127], replicated
The draws below stay inside these ranges and needn't reach their ends.
All inputs are finite; a program needn't handle non-finite values. No bound on the sum of `brain_mask` on one device may be relied on, other than what follows from the above.
Results may differ from the reference program's by a relative error of at most 0.00095.
Values may be sent and summed in bfloat16 or wider, within the bound.
A program may use at most 128 MiB of HBM per device.

```python
import math
import jax
import jax.numpy as jnp
from jax import lax

FR = 128
RAD = 4
CX = 8
CY = 8
CZ = 128
NX = 32
NY = 64
NZ = 128


def draw_movie(key, part):
    key_shift = jax.random.fold_in(key, 11)
    key_amp = jax.random.fold_in(key, 12)
    key_sign = jax.random.fold_in(key, 13)
    key_phase = jax.random.fold_in(key, 14)
    key_noise = jax.random.fold_in(key, 15)
    key_smooth = jax.random.fold_in(key, 16)
    key_heading = jax.random.fold_in(key, 17)
    key_offset = jax.random.fold_in(key, 18)
    half_frames = FR // 2
    columns = NY // CY
    shift = jax.random.randint(key_shift, (), 0, half_frames)
    brick_x = jnp.arange(NX) // CX
    brick_y = jnp.arange(NY) // CY
    brick = brick_x[:, None] * columns + brick_y[None, :]
    freq_index = ((brick + shift) % half_frames).astype(jnp.float32)
    omega = math.pi * (freq_index + 0.5) / half_frames
    rise = brick_y.astype(jnp.float32) / max(columns - 1, 1)
    scale_col = jnp.exp(math.log(3.0) * rise)
    amp = jax.random.uniform(key_amp, (NX, NY, NZ), jnp.float32, 0.5, 1.5)
    noise = 0.4 * jnp.clip(jax.random.normal(key_noise, (NX, NY, NZ, FR), jnp.float32), -3.0, 3.0)
    sign = 2.0 * jax.random.bernoulli(key_sign, 0.5, (NX, NY, NZ)).astype(jnp.float32) - 1.0
    phase = jax.random.uniform(key_phase, (NX, NY, NZ), jnp.float32, -math.pi, math.pi)
    times = jnp.arange(FR).astype(jnp.float32)
    wave = jnp.cos(omega[:, :, None, None] * times[None, None, None, :] + phase[:, :, :, None])
    slow_index = jax.random.randint(key_smooth, (), 0, half_frames).astype(jnp.float32)
    slow_omega = math.pi * (slow_index + 0.25) / half_frames
    heading = 2.0 * jax.random.bernoulli(key_heading, 0.5, (3,)).astype(jnp.float32) - 1.0
    offset = jax.random.uniform(key_offset, (), jnp.float32, -math.pi, math.pi)
    across = 2.0 * math.pi / (8.0 * RAD)
    along = 2.0 * math.pi / (16.0 * RAD)
    pos_x = jnp.arange(NX).astype(jnp.float32)
    pos_y = jnp.arange(NY).astype(jnp.float32)
    pos_z = jnp.arange(NZ).astype(jnp.float32)
    spatial = heading[0] * across * pos_x[:, None, None] + heading[1] * across * pos_y[None, :, None] + heading[2] * along * pos_z[None, None, :] + offset
    smooth_part = 1.2 * jnp.cos(spatial[:, :, :, None] + slow_omega * times[None, None, None, :])
    value = scale_col[None, :, None, None] * (1.5 * (amp * sign)[:, :, :, None] * wave + noise + smooth_part)
    return value.astype(jnp.bfloat16)


def set_ends(entries, stream_key, smallest, largest):
    spot = [jax.random.randint(jax.random.fold_in(stream_key, axis), (), 0, length) for axis, length in enumerate(entries.shape)]
    widest = entries.shape.index(max(entries.shape))
    neighbour = spot[:widest] + [(spot[widest] + 1) % entries.shape[widest]] + spot[widest + 1:]
    return entries.at[tuple(spot)].set(smallest).at[tuple(neighbour)].set(largest)


def setup_inputs(seed: int = 0) -> dict:
    streams_of = jax.random.split(jax.random.key(seed), 3)
    return {
        "movie": draw_movie(jax.random.fold_in(streams_of[2], 71), 0),
        "brain_mask": set_ends((jax.random.randint(streams_of[1], (NX, NY, NZ), 0, 4) < 3).astype(jnp.int32), jax.random.fold_in(streams_of[1], 1), 0, 1),
    }


def kernel_weights():
    offsets = jnp.arange(-RAD, RAD + 1).astype(jnp.float32)
    sigma = RAD / 2.0
    raw = jnp.exp(-offsets * offsets / (2.0 * sigma * sigma))
    return raw / jnp.sum(raw)

def blur_axis(field, axis, weights, length):
    widths = [(0, 0)] * field.ndim
    widths[axis] = (RAD, RAD)
    padded = jnp.pad(field, widths)
    total = jnp.zeros(field.shape, jnp.float32)
    for k in range(2 * RAD + 1):
        total = total + weights[k] * lax.slice_in_dim(padded, k, k + length, axis=axis)
    return total

def chol_solve(factor, right):
    middle = lax.linalg.triangular_solve(factor, right, left_side=True, lower=True)
    return lax.linalg.triangular_solve(factor, middle, left_side=True, lower=True, transpose_a=True)

def reference(movie, brain_mask):
    weights = kernel_weights()
    nblk = FR // 8
    blocks = jnp.moveaxis(movie.reshape(NX, NY, NZ, nblk, 8), 3, 0)
    mask_f = brain_mask.astype(jnp.float32)[:, :, :, None]

    def filter_block(block):
        field = block.astype(jnp.float32)
        blur = blur_axis(field, 2, weights, NZ)
        blur = blur_axis(blur, 1, weights, NY)
        blur = blur_axis(blur, 0, weights, NX)
        return mask_f * (field - blur)
    filtered = lax.map(filter_block, blocks)
    filtered = jnp.moveaxis(filtered, 0, 3).reshape(NX * NY * NZ, FR)
    rows_blk = CX * CY * CZ
    row_blocks = filtered.reshape(-1, rows_blk, FR)

    def add_gram(total, rows):
        part = lax.dot_general(rows.astype(jnp.float32), rows.astype(jnp.float32), (((0,), (0,)), ((), ())), precision=lax.Precision.HIGHEST, preferred_element_type=jnp.float32)
        return (total + part, None)
    gram, _ = lax.scan(add_gram, jnp.zeros((FR, FR), jnp.float32), row_blocks)
    g_left = gram[:FR - 1, :FR - 1]
    g_right = gram[:FR - 1, 1:]
    lam = 0.5 * jnp.trace(g_left) / (FR - 1)
    factor = jnp.linalg.cholesky(g_left + lam * jnp.eye(FR - 1, dtype=jnp.float32))
    propagator = chol_solve(factor, g_right)
    advance = jnp.zeros((FR, FR), jnp.float32)
    advance = advance.at[0, 0].set(1.0)
    advance = advance.at[:FR - 1, 1:].set(propagator)

    def fit_block(rows):
        return jnp.dot(rows.astype(jnp.float32), advance.astype(jnp.float32), precision=lax.Precision.HIGHEST, preferred_element_type=jnp.float32).astype(jnp.bfloat16)
    fitted = lax.map(fit_block, row_blocks).reshape(NX, NY, NZ, FR)
    return (fitted, propagator)
```

```python
import functools

import numpy as np
import jax
import jax.numpy as jnp
from jax import lax
from jax.experimental import pallas as pl
from jax.experimental.pallas import tpu as pltpu
from jax.sharding import PartitionSpec as P

RAD = 4
MESH = pl.DeviceIdType.MESH
F32 = jnp.float32
BF16 = jnp.bfloat16


def weights():
    k = np.arange(-RAD, RAD + 1).astype(np.float32)
    sigma = RAD / 2.0
    raw = np.exp(-k * k / np.float32(2.0 * sigma * sigma)).astype(np.float32)
    w = raw / raw.sum(dtype=np.float32)
    return [float(w[RAD + j]) for j in range(RAD + 1)]


W = weights()


def blur9(items, at):
    total = W[0] * items[at + RAD]
    for k in range(1, RAD + 1):
        total = total + W[k] * (items[at + RAD - k] + items[at + RAD + k])
    return total


def split(v):
    hi = v.astype(BF16)
    return hi, (v - hi.astype(F32)).astype(BF16)


def filter_kernel(
    nx, ny,
    movie, mask, filt, gram_out,
    ylo, yhi, ysend, xlo, xhi, yb, xb, band, maskt, gacc, gpart, rsbuf, xbuf, gfull,
    ysl, ysh, yrl, yrh, xsl, xsh, xrl, xrh, s1, r1, s2, r2, s3, r3,
):
    cx, cy, cz, fr = movie.shape
    gx, gy = lax.axis_index("gx"), lax.axis_index("gy")
    barrier = pltpu.get_barrier_semaphore()

    def hello_y(d, c):
        pl.semaphore_signal(barrier, inc=1, device_id=(gx, lax.rem(gy + d, ny)), device_id_type=MESH)
        return c

    def hello_x(d, c):
        pl.semaphore_signal(barrier, inc=1, device_id=(lax.rem(gx + d, nx), gy), device_id_type=MESH)
        return c

    lax.fori_loop(1, ny, hello_y, 0)
    lax.fori_loop(1, nx, hello_x, 0)
    pl.semaphore_wait(barrier, ny - 1 + nx - 1)

    has_yl, has_yh = gy > 0, gy < ny - 1
    has_xl, has_xh = gx > 0, gx < nx - 1

    def order(i):
        return jnp.where(i % 2 == 0, i // 2, cx - 1 - i // 2)

    def y_up(l):
        return pltpu.make_async_remote_copy(
            src_ref=movie.at[l, pl.ds(cy - RAD, RAD)], dst_ref=ylo.at[l],
            send_sem=ysl.at[l], recv_sem=yrl.at[l],
            device_id=(gx, gy + 1), device_id_type=MESH)

    def y_down(l):
        return pltpu.make_async_remote_copy(
            src_ref=movie.at[l, pl.ds(0, RAD)], dst_ref=yhi.at[l],
            send_sem=ysh.at[l], recv_sem=yrh.at[l],
            device_id=(gx, gy - 1), device_id_type=MESH)

    def x_up(j):
        return pltpu.make_async_remote_copy(
            src_ref=ysend.at[cx - RAD + j], dst_ref=xlo.at[j],
            send_sem=xsl.at[j], recv_sem=xrl.at[j],
            device_id=(gx + 1, gy), device_id_type=MESH)

    def x_down(j):
        return pltpu.make_async_remote_copy(
            src_ref=ysend.at[j], dst_ref=xhi.at[j],
            send_sem=xsh.at[j], recv_sem=xrh.at[j],
            device_id=(gx - 1, gy), device_id_type=MESH)

    def start_y(i, c):
        l = order(i)

        @pl.when(has_yh)
        def _():
            y_up(l).start()

        @pl.when(has_yl)
        def _():
            y_down(l).start()
        return c

    lax.fori_loop(0, cx, start_y, 0)

    @pl.when(jnp.logical_not(has_yl))
    def _():
        ylo[...] = jnp.zeros_like(ylo)

    @pl.when(jnp.logical_not(has_yh))
    def _():
        yhi[...] = jnp.zeros_like(yhi)

    @pl.when(jnp.logical_not(has_xl))
    def _():
        xlo[...] = jnp.zeros_like(xlo)

    @pl.when(jnp.logical_not(has_xh))
    def _():
        xhi[...] = jnp.zeros_like(xhi)

    dist = jnp.abs(lax.broadcasted_iota(jnp.int32, (cz, cz), 0) - lax.broadcasted_iota(jnp.int32, (cz, cz), 1))
    t = jnp.zeros((cz, cz), F32)
    for k in range(RAD + 1):
        t = jnp.where(dist == k, W[k], t)
    th, tl = split(t)
    band[:, 0:cz] = th
    band[:, cz:2 * cz] = tl
    band[:, 2 * cz:3 * cz] = th
    maskt[...] = jnp.transpose(mask[...].astype(F32).reshape(cx * cy, cz)).astype(BF16)
    gacc[...] = jnp.zeros_like(gacc)

    ZT = 16

    def y_layer(i, c):
        l = order(i)

        @pl.when(has_yl)
        def _():
            y_up(l).wait_recv()

        @pl.when(has_yh)
        def _():
            y_down(l).wait_recv()

        def tile(z, c2):
            rows = pl.ds(pl.multiple_of(z * ZT, ZT), ZT)
            items = [ylo[l, k, rows, :].astype(F32) for k in range(RAD)]
            items += [movie[l, k, rows, :].astype(F32) for k in range(cy)]
            items += [yhi[l, k, rows, :].astype(F32) for k in range(RAD)]
            for y in range(cy):
                v = blur9(items, y)
                yb[l + RAD, y, rows, :] = v
                ysend[l, y, rows, :] = v.astype(BF16)
            return c2

        lax.fori_loop(0, cz // ZT, tile, 0)

        @pl.when(jnp.logical_and(i % 2 == 0, has_xl))
        def _():
            x_down(i // 2).start()

        @pl.when(jnp.logical_and(i % 2 == 1, has_xh))
        def _():
            x_up(RAD - 1 - i // 2).start()
        return c

    lax.fori_loop(0, cx, y_layer, 0)

    def widen(src, j, to):
        def tile(z, c):
            rows = pl.ds(pl.multiple_of(z * ZT, ZT), ZT)
            for y in range(cy):
                yb[to, y, rows, :] = src[j, y, rows, :].astype(F32)
            return c
        lax.fori_loop(0, cz // ZT, tile, 0)

    def x_layer(l):
        def tile(z, c):
            rows = pl.ds(pl.multiple_of(z * ZT, ZT), ZT)
            for y in range(cy):
                items = [yb[l + k, y, rows, :] for k in range(2 * RAD + 1)]
                xb[y, rows, :] = blur9(items, 0)
            return c
        lax.fori_loop(0, cz // ZT, tile, 0)
        lanes = lax.broadcasted_iota(jnp.int32, (cx * cy, fr), 0)
        for y in range(0, cy, 2):
            parts = [split(xb[y + k]) for k in range(2)]
            hi = jnp.concatenate([p[0] for p in parts], axis=1)
            lo = jnp.concatenate([p[1] for p in parts], axis=1)
            blur = jnp.dot(band[...], jnp.concatenate([hi, hi, lo], axis=0), preferred_element_type=F32)
            left, right = [], []
            for k in range(2):
                one = jnp.where(lanes == l * cy + y + k, 1.0, 0.0).astype(BF16)
                m = jnp.dot(maskt[...], one, preferred_element_type=F32)
                f = m * (movie[l, y + k].astype(F32) - blur[:, k * fr:(k + 1) * fr])
                fh, fl = split(f)
                both = jnp.concatenate([fh, fl], axis=1)
                filt[l, y + k] = both
                left.append(fh)
                right.append(both)
            gacc[...] += lax.dot_general(
                jnp.concatenate(left, axis=0), jnp.concatenate(right, axis=0),
                (((0,), (0,)), ((), ())), preferred_element_type=F32)

    def x_step(j, c):
        @pl.when(has_xl)
        def _():
            x_up(RAD - 1 - j).wait_recv()

        @pl.when(has_xh)
        def _():
            x_down(j).wait_recv()
        widen(xlo, RAD - 1 - j, RAD - 1 - j)
        widen(xhi, j, cx + RAD + j)

        def two(s, c2):
            x_layer(jnp.where(s == 0, RAD - 1 - j, cx - RAD + j))
            return c2
        lax.fori_loop(0, 2, two, 0)
        return c

    lax.fori_loop(0, RAD, x_step, 0)

    g = gacc[:, 0:fr] + gacc[:, fr:2 * fr] + jnp.transpose(gacc[:, fr:2 * fr])
    r = fr // ny
    for p in range(ny):
        gpart[p] = g[p * r:(p + 1) * r]

    def scatter(d):
        to = lax.rem(gy + d, ny)
        return pltpu.make_async_remote_copy(
            src_ref=gpart.at[to], dst_ref=rsbuf.at[d], send_sem=s1.at[d], recv_sem=r1.at[d],
            device_id=(gx, to), device_id_type=MESH)

    def across(d):
        return pltpu.make_async_remote_copy(
            src_ref=xbuf.at[gx], dst_ref=xbuf.at[gx], send_sem=s2.at[d], recv_sem=r2.at[d],
            device_id=(lax.rem(gx + d, nx), gy), device_id_type=MESH)

    def gather(d):
        return pltpu.make_async_remote_copy(
            src_ref=gfull.at[gy], dst_ref=gfull.at[gy], send_sem=s3.at[d], recv_sem=r3.at[d],
            device_id=(gx, lax.rem(gy + d, ny)), device_id_type=MESH)

    def each(n, f):
        def body(d, c):
            f(d)
            return c
        lax.fori_loop(1, n, body, 0)

    each(ny, lambda d: scatter(d).start())
    each(ny, lambda d: scatter(d).wait_recv())
    total = gpart[gy]
    for d in range(1, ny):
        total = total + rsbuf[d]
    xbuf[gx] = total
    each(nx, lambda d: across(d).start())
    each(nx, lambda d: across(d).wait_recv())
    total = xbuf[0]
    for d in range(1, nx):
        total = total + xbuf[d]
    gfull[gy] = total
    each(ny, lambda d: gather(d).start())
    each(ny, lambda d: gather(d).wait_recv())
    gram_out[...] = gfull[...]

    each(ny, lambda d: scatter(d).wait_send())
    each(nx, lambda d: across(d).wait_send())
    each(ny, lambda d: gather(d).wait_send())

    def drain_y(l, c):
        @pl.when(has_yh)
        def _():
            y_up(l).wait_send()

        @pl.when(has_yl)
        def _():
            y_down(l).wait_send()
        return c

    def drain_x(j, c):
        @pl.when(has_xh)
        def _():
            x_up(j).wait_send()

        @pl.when(has_xl)
        def _():
            x_down(j).wait_send()
        return c

    lax.fori_loop(0, cx, drain_y, 0)
    lax.fori_loop(0, RAD, drain_x, 0)


def fit_kernel(gram, filt, out, prop, a, b, m):
    fr = gram.shape[0]

    @pl.when(pl.program_id(0) == 0)
    def _():
        g = gram[...]
        row = lax.broadcasted_iota(jnp.int32, (fr, fr), 0)
        col = lax.broadcasted_iota(jnp.int32, (fr, fr), 1)
        diag = jnp.where((row == col) & (row < fr - 1), g, 0.0)
        lam = 0.5 * jnp.sum(diag) / (fr - 1)
        last = (row == fr - 1) | (col == fr - 1)
        a[...] = jnp.where(last, 0.0, g) + jnp.where(row == col, lam, 0.0)
        b[...] = jnp.where(row == fr - 1, 0.0, g)

        def block(i, c):
            group = pl.ds(pl.multiple_of(i * 8, 8), 8)
            sub = lax.broadcasted_iota(jnp.int32, (8, fr), 0)
            for s in range(0, 8, 2):
                ga, gb = a[group, :], b[group, :]
                a0, a1 = ga[s:s + 1], ga[s + 1:s + 2]
                b0, b1 = gb[s:s + 1], gb[s + 1:s + 2]
                p, q = a0[:, s:s + 1], a0[:, s + 1:s + 2]
                q2, r = a1[:, s:s + 1], a1[:, s + 1:s + 2]
                inv = 1.0 / (p * r - q * q2)
                p, q, q2, r = p * inv, q * inv, q2 * inv, r * inv
                na0, na1 = r * a0 - q * a1, p * a1 - q2 * a0
                nb0, nb1 = r * b0 - q * b1, p * b1 - q2 * b0
                old = a[...]
                c0, c1 = old[:, s:s + 1], old[:, s + 1:s + 2]
                a[...] = old - c0 * na0 - c1 * na1
                b[...] = b[...] - c0 * nb0 - c1 * nb1
                a[group, :] = jnp.where(sub == s, na0, jnp.where(sub == s + 1, na1, a[group, :]))
                b[group, :] = jnp.where(sub == s, nb0, jnp.where(sub == s + 1, nb1, b[group, :]))
            a[...] = pltpu.roll(a[...], fr - 8, 1)
            return c

        lax.fori_loop(0, fr // 8, block, 0)
        x = b[...]
        prop[...] = x[0:fr - 1, 1:fr]
        adv = jnp.where(col == 0, jnp.where(row == 0, 1.0, 0.0), x)
        mh, ml = split(adv)
        m[0:fr, 0:fr] = mh
        m[0:fr, fr:2 * fr] = ml
        m[fr:2 * fr, 0:fr] = mh
        m[fr:2 * fr, fr:2 * fr] = jnp.zeros((fr, fr), BF16)

    for y in range(filt.shape[1]):
        v = jnp.dot(filt[0, y], m[...], preferred_element_type=F32)
        out[0, y] = (v[:, 0:fr] + v[:, fr:2 * fr]).astype(BF16)


def on_device(nx, ny, movie, brain_mask):
    cx, cy, cz, fr = movie.shape
    r = fr // ny
    vmem = pl.BlockSpec(memory_space=pltpu.VMEM)
    dma = pltpu.SemaphoreType.DMA
    filt, gram = pl.pallas_call(
        functools.partial(filter_kernel, nx, ny),
        out_shape=(
            jax.ShapeDtypeStruct((cx, cy, cz, 2 * fr), BF16),
            jax.ShapeDtypeStruct((ny, r, fr), F32),
        ),
        in_specs=[vmem, vmem],
        out_specs=(vmem, vmem),
        scratch_shapes=[
            pltpu.VMEM((cx, RAD, cz, fr), BF16),
            pltpu.VMEM((cx, RAD, cz, fr), BF16),
            pltpu.VMEM((cx, cy, cz, fr), BF16),
            pltpu.VMEM((RAD, cy, cz, fr), BF16),
            pltpu.VMEM((RAD, cy, cz, fr), BF16),
            pltpu.VMEM((cx + 2 * RAD, cy, cz, fr), F32),
            pltpu.VMEM((cy, cz, fr), F32),
            pltpu.VMEM((cz, 3 * cz), BF16),
            pltpu.VMEM((cz, cx * cy), BF16),
            pltpu.VMEM((fr, 2 * fr), F32),
            pltpu.VMEM((ny, r, fr), F32),
            pltpu.VMEM((ny, r, fr), F32),
            pltpu.VMEM((nx, r, fr), F32),
            pltpu.VMEM((ny, r, fr), F32),
            dma((cx,)), dma((cx,)), dma((cx,)), dma((cx,)),
            dma((RAD,)), dma((RAD,)), dma((RAD,)), dma((RAD,)),
            dma((ny,)), dma((ny,)), dma((nx,)), dma((nx,)), dma((ny,)), dma((ny,)),
        ],
        compiler_params=pltpu.CompilerParams(
            collective_id=0, has_side_effects=True, vmem_limit_bytes=48 * 1024 * 1024),
    )(movie, brain_mask)
    gram = gram.reshape(fr, fr)
    fitted, propagator = pl.pallas_call(
        fit_kernel,
        grid=(cx,),
        out_shape=(
            jax.ShapeDtypeStruct((cx, cy, cz, fr), BF16),
            jax.ShapeDtypeStruct((fr - 1, fr - 1), F32),
        ),
        in_specs=[
            pl.BlockSpec((fr, fr), lambda i: (0, 0)),
            pl.BlockSpec((1, cy, cz, 2 * fr), lambda i: (i, 0, 0, 0)),
        ],
        out_specs=(
            pl.BlockSpec((1, cy, cz, fr), lambda i: (i, 0, 0, 0)),
            pl.BlockSpec((fr - 1, fr - 1), lambda i: (0, 0)),
        ),
        scratch_shapes=[
            pltpu.VMEM((fr, fr), F32),
            pltpu.VMEM((fr, fr), F32),
            pltpu.VMEM((2 * fr, 2 * fr), BF16),
        ],
        compiler_params=pltpu.CompilerParams(vmem_limit_bytes=32 * 1024 * 1024),
    )(gram, filt)
    return fitted, propagator


def solution(mesh):
    nx, ny = mesh.shape["gx"], mesh.shape["gy"]
    return jax.shard_map(
        functools.partial(on_device, nx, ny),
        mesh=mesh,
        in_specs=(P("gx", "gy", None, None), P("gx", "gy", None)),
        out_specs=(P("gx", "gy", None, None), P()),
        check_vma=False,
    )
```

```python
import functools

import numpy as np
import jax
import jax.numpy as jnp
from jax import lax
from jax.experimental import pallas as pl
from jax.experimental.pallas import tpu as pltpu
from jax.sharding import PartitionSpec as P

RAD = 4
MESH = pl.DeviceIdType.MESH
F32 = jnp.float32
BF16 = jnp.bfloat16


def weights():
    k = np.arange(-RAD, RAD + 1).astype(np.float32)
    sigma = RAD / 2.0
    raw = np.exp(-k * k / np.float32(2.0 * sigma * sigma)).astype(np.float32)
    w = raw / raw.sum(dtype=np.float32)
    return [float(w[RAD + j]) for j in range(RAD + 1)]


W = weights()


def blur9(items, at):
    total = W[0] * items[at + RAD]
    for k in range(1, RAD + 1):
        total = total + W[k] * (items[at + RAD - k] + items[at + RAD + k])
    return total


def split(v):
    hi = v.astype(BF16)
    return hi, (v - hi.astype(F32)).astype(BF16)


def filter_kernel(
    nx, ny,
    movie_hbm, mask_hbm, filt, gram_out,
    movie, mask, local, ylo, yhi, ysend, xlo, xhi, yb, xb, band, maskt, gacc, gpart, rsbuf, xbuf, gfull,
    ysl, ysh, yrl, yrh, xsl, xsh, xrl, xrh, s1, r1, s2, r2, s3, r3,
):
    cx, cy, cz, fr = movie.shape
    gx, gy = lax.axis_index("gx"), lax.axis_index("gy")
    load_movie = pltpu.make_async_copy(movie_hbm, movie, local.at[0])
    load_mask = pltpu.make_async_copy(mask_hbm, mask, local.at[1])
    load_movie.start()
    load_mask.start()
    barrier = pltpu.get_barrier_semaphore()

    def hello_y(d, c):
        pl.semaphore_signal(barrier, inc=1, device_id=(gx, lax.rem(gy + d, ny)), device_id_type=MESH)
        return c

    def hello_x(d, c):
        pl.semaphore_signal(barrier, inc=1, device_id=(lax.rem(gx + d, nx), gy), device_id_type=MESH)
        return c

    lax.fori_loop(1, ny, hello_y, 0)
    lax.fori_loop(1, nx, hello_x, 0)
    pl.semaphore_wait(barrier, ny - 1 + nx - 1)

    has_yl, has_yh = gy > 0, gy < ny - 1
    has_xl, has_xh = gx > 0, gx < nx - 1

    def order(i):
        return jnp.where(i % 2 == 0, i // 2, cx - 1 - i // 2)

    def y_up(l):
        return pltpu.make_async_remote_copy(
            src_ref=movie_hbm.at[l, pl.ds(cy - RAD, RAD)], dst_ref=ylo.at[l],
            send_sem=ysl.at[l], recv_sem=yrl.at[l],
            device_id=(gx, gy + 1), device_id_type=MESH)

    def y_down(l):
        return pltpu.make_async_remote_copy(
            src_ref=movie_hbm.at[l, pl.ds(0, RAD)], dst_ref=yhi.at[l],
            send_sem=ysh.at[l], recv_sem=yrh.at[l],
            device_id=(gx, gy - 1), device_id_type=MESH)

    def x_up(j):
        return pltpu.make_async_remote_copy(
            src_ref=ysend.at[cx - RAD + j], dst_ref=xlo.at[j],
            send_sem=xsl.at[j], recv_sem=xrl.at[j],
            device_id=(gx + 1, gy), device_id_type=MESH)

    def x_down(j):
        return pltpu.make_async_remote_copy(
            src_ref=ysend.at[j], dst_ref=xhi.at[j],
            send_sem=xsh.at[j], recv_sem=xrh.at[j],
            device_id=(gx - 1, gy), device_id_type=MESH)

    def start_y(i, c):
        l = order(i)

        @pl.when(has_yh)
        def _():
            y_up(l).start()

        @pl.when(has_yl)
        def _():
            y_down(l).start()
        return c

    lax.fori_loop(0, cx, start_y, 0)

    @pl.when(jnp.logical_not(has_yl))
    def _():
        ylo[...] = jnp.zeros_like(ylo)

    @pl.when(jnp.logical_not(has_yh))
    def _():
        yhi[...] = jnp.zeros_like(yhi)

    @pl.when(jnp.logical_not(has_xl))
    def _():
        xlo[...] = jnp.zeros_like(xlo)

    @pl.when(jnp.logical_not(has_xh))
    def _():
        xhi[...] = jnp.zeros_like(xhi)

    dist = jnp.abs(lax.broadcasted_iota(jnp.int32, (cz, cz), 0) - lax.broadcasted_iota(jnp.int32, (cz, cz), 1))
    t = jnp.zeros((cz, cz), F32)
    for k in range(RAD + 1):
        t = jnp.where(dist == k, W[k], t)
    th, tl = split(t)
    band[:, 0:cz] = th
    band[:, cz:2 * cz] = tl
    band[:, 2 * cz:3 * cz] = th
    load_mask.wait()
    maskt[...] = jnp.transpose(mask[...].astype(F32).reshape(cx * cy, cz)).astype(BF16)
    gacc[...] = jnp.zeros_like(gacc)

    load_movie.wait()
    ZT = 16

    def y_layer(i, c):
        l = order(i)

        @pl.when(has_yl)
        def _():
            y_up(l).wait_recv()

        @pl.when(has_yh)
        def _():
            y_down(l).wait_recv()

        def tile(z, c2):
            rows = pl.ds(pl.multiple_of(z * ZT, ZT), ZT)
            items = [ylo[l, k, rows, :].astype(F32) for k in range(RAD)]
            items += [movie[l, k, rows, :].astype(F32) for k in range(cy)]
            items += [yhi[l, k, rows, :].astype(F32) for k in range(RAD)]
            for y in range(cy):
                v = blur9(items, y)
                yb[l + RAD, y, rows, :] = v
                ysend[l, y, rows, :] = v.astype(BF16)
            return c2

        lax.fori_loop(0, cz // ZT, tile, 0)

        @pl.when(jnp.logical_and(i % 2 == 0, has_xl))
        def _():
            x_down(i // 2).start()

        @pl.when(jnp.logical_and(i % 2 == 1, has_xh))
        def _():
            x_up(RAD - 1 - i // 2).start()
        return c

    lax.fori_loop(0, cx, y_layer, 0)

    def widen(src, j, to):
        def tile(z, c):
            rows = pl.ds(pl.multiple_of(z * ZT, ZT), ZT)
            for y in range(cy):
                yb[to, y, rows, :] = src[j, y, rows, :].astype(F32)
            return c
        lax.fori_loop(0, cz // ZT, tile, 0)

    def x_layer(l):
        def tile(z, c):
            rows = pl.ds(pl.multiple_of(z * ZT, ZT), ZT)
            for y in range(cy):
                items = [yb[l + k, y, rows, :] for k in range(2 * RAD + 1)]
                xb[y, rows, :] = blur9(items, 0)
            return c
        lax.fori_loop(0, cz // ZT, tile, 0)
        lanes = lax.broadcasted_iota(jnp.int32, (cx * cy, fr), 0)
        for y in range(0, cy, 2):
            parts = [split(xb[y + k]) for k in range(2)]
            hi = jnp.concatenate([p[0] for p in parts], axis=1)
            lo = jnp.concatenate([p[1] for p in parts], axis=1)
            blur = jnp.dot(band[...], jnp.concatenate([hi, hi, lo], axis=0), preferred_element_type=F32)
            left, right = [], []
            for k in range(2):
                one = jnp.where(lanes == l * cy + y + k, 1.0, 0.0).astype(BF16)
                m = jnp.dot(maskt[...], one, preferred_element_type=F32)
                f = m * (movie[l, y + k].astype(F32) - blur[:, k * fr:(k + 1) * fr])
                fh, fl = split(f)
                both = jnp.concatenate([fh, fl], axis=1)
                filt[l, y + k] = both
                left.append(fh)
                right.append(both)
            gacc[...] += lax.dot_general(
                jnp.concatenate(left, axis=0), jnp.concatenate(right, axis=0),
                (((0,), (0,)), ((), ())), preferred_element_type=F32)

    def x_step(j, c):
        @pl.when(has_xl)
        def _():
            x_up(RAD - 1 - j).wait_recv()

        @pl.when(has_xh)
        def _():
            x_down(j).wait_recv()
        widen(xlo, RAD - 1 - j, RAD - 1 - j)
        widen(xhi, j, cx + RAD + j)

        def two(s, c2):
            x_layer(jnp.where(s == 0, RAD - 1 - j, cx - RAD + j))
            return c2
        lax.fori_loop(0, 2, two, 0)
        return c

    lax.fori_loop(0, RAD, x_step, 0)

    g = gacc[:, 0:fr] + gacc[:, fr:2 * fr] + jnp.transpose(gacc[:, fr:2 * fr])
    r = fr // ny
    for p in range(ny):
        gpart[p] = g[p * r:(p + 1) * r]

    def scatter(d):
        to = lax.rem(gy + d, ny)
        return pltpu.make_async_remote_copy(
            src_ref=gpart.at[to], dst_ref=rsbuf.at[d], send_sem=s1.at[d], recv_sem=r1.at[d],
            device_id=(gx, to), device_id_type=MESH)

    def across(d):
        return pltpu.make_async_remote_copy(
            src_ref=xbuf.at[gx], dst_ref=xbuf.at[gx], send_sem=s2.at[d], recv_sem=r2.at[d],
            device_id=(lax.rem(gx + d, nx), gy), device_id_type=MESH)

    def gather(d):
        return pltpu.make_async_remote_copy(
            src_ref=gfull.at[gy], dst_ref=gfull.at[gy], send_sem=s3.at[d], recv_sem=r3.at[d],
            device_id=(gx, lax.rem(gy + d, ny)), device_id_type=MESH)

    def each(n, f):
        def body(d, c):
            f(d)
            return c
        lax.fori_loop(1, n, body, 0)

    each(ny, lambda d: scatter(d).start())
    each(ny, lambda d: scatter(d).wait_recv())
    total = gpart[gy]
    for d in range(1, ny):
        total = total + rsbuf[d]
    xbuf[gx] = total
    each(nx, lambda d: across(d).start())
    each(nx, lambda d: across(d).wait_recv())
    total = xbuf[0]
    for d in range(1, nx):
        total = total + xbuf[d]
    gfull[gy] = total
    each(ny, lambda d: gather(d).start())
    each(ny, lambda d: gather(d).wait_recv())
    gram_out[...] = gfull[...]

    each(ny, lambda d: scatter(d).wait_send())
    each(nx, lambda d: across(d).wait_send())
    each(ny, lambda d: gather(d).wait_send())

    def drain_y(l, c):
        @pl.when(has_yh)
        def _():
            y_up(l).wait_send()

        @pl.when(has_yl)
        def _():
            y_down(l).wait_send()
        return c

    def drain_x(j, c):
        @pl.when(has_xh)
        def _():
            x_up(j).wait_send()

        @pl.when(has_xl)
        def _():
            x_down(j).wait_send()
        return c

    lax.fori_loop(0, cx, drain_y, 0)
    lax.fori_loop(0, RAD, drain_x, 0)


BLK = 8


def sweep_block(a, dbuf, zbuf, start):
    n = a.shape[0]
    row = lax.broadcasted_iota(jnp.int32, (n, n), 1)
    lane = lax.broadcasted_iota(jnp.int32, (BLK, n), 1)
    sub = lax.broadcasted_iota(jnp.int32, (BLK, n), 0)
    inside = (lane >= start) & (lane < start + BLK)
    panel = a[start:start + BLK, :]
    u = jnp.where(inside, 0.0, panel)
    zbuf[...] = jnp.where(lane == start + sub, -1.0, u)
    for j in range(BLK):
        dbuf[j] = jnp.broadcast_to(panel[:, start + j:start + j + 1], (BLK, n))
    d = {(i, j): jnp.broadcast_to(dbuf[j, i:i + 1, :], (BLK, n)) for j in range(BLK) for i in range(j + 1)}
    z = [jnp.broadcast_to(zbuf[i:i + 1, :], (BLK, n)) for i in range(BLK)]
    inverses, multipliers = {}, {}
    for s in range(0, BLK, 2):
        p, q, r = d[s, s], d[s, s + 1], d[s + 1, s + 1]
        inv = 1.0 / (p * r - q * q)
        ip, iq, ir = r * inv, -(q * inv), p * inv
        inverses[s] = (ip, iq, ir)
        for i in range(s + 2, BLK):
            m0 = d[s, i] * ip + d[s + 1, i] * iq
            m1 = d[s, i] * iq + d[s + 1, i] * ir
            multipliers[s, i] = (m0, m1)
            for j in range(i, BLK):
                d[i, j] = d[i, j] - (m0 * d[s, j] + m1 * d[s + 1, j])
            z[i] = z[i] - (m0 * z[s] + m1 * z[s + 1])
    for s in range(BLK - 2, -1, -2):
        ip, iq, ir = inverses[s]
        w0, w1 = ip * z[s] + iq * z[s + 1], iq * z[s] + ir * z[s + 1]
        for i in range(BLK - 1, s + 1, -1):
            m0, m1 = multipliers[s, i]
            w0, w1 = w0 - m0 * z[i], w1 - m1 * z[i]
        z[s], z[s + 1] = w0, w1
    full = z[0]
    for i in range(1, BLK):
        full = jnp.where(sub == i, z[i], full)
    update = lax.dot_general(
        u, full, (((0,), (0,)), ((), ())), precision=lax.Precision.HIGHEST, preferred_element_type=F32)
    a[...] = jnp.where((row >= start) & (row < start + BLK), 0.0, a[...]) - update
    a[start:start + BLK, :] = full


def fit_kernel(gram, filt, out, prop, a, m, dbuf, zbuf):
    fr = gram.shape[0]

    @pl.when(pl.program_id(0) == 0)
    def _():
        g = gram[...]
        row = lax.broadcasted_iota(jnp.int32, (fr, fr), 0)
        col = lax.broadcasted_iota(jnp.int32, (fr, fr), 1)
        diag = jnp.where((row == col) & (row < fr - 1), g, 0.0)
        lam = 0.5 * jnp.sum(diag) / (fr - 1)
        scaled = g / lam
        last = (row == fr - 1) | (col == fr - 1)
        a[...] = jnp.where(last, 0.0, scaled) + jnp.where(row == col, 1.0, 0.0)
        for start in range(0, fr, BLK):
            sweep_block(a, dbuf, zbuf, start)
        x = -jnp.dot(a[...], jnp.where(row == fr - 1, 0.0, scaled),
                     precision=lax.Precision.HIGHEST, preferred_element_type=F32)
        prop[...] = x[0:fr - 1, 1:fr]
        adv = jnp.where(col == 0, jnp.where(row == 0, 1.0, 0.0), x)
        mh, ml = split(adv)
        m[0:fr, 0:fr] = mh
        m[0:fr, fr:2 * fr] = ml
        m[fr:2 * fr, 0:fr] = mh
        m[fr:2 * fr, fr:2 * fr] = jnp.zeros((fr, fr), BF16)

    i = pl.program_id(0)
    for y in range(filt.shape[1]):
        v = jnp.dot(filt[i, y], m[...], preferred_element_type=F32)
        out[0, y] = (v[:, 0:fr] + v[:, fr:2 * fr]).astype(BF16)


def on_device(nx, ny, movie, brain_mask):
    cx, cy, cz, fr = movie.shape
    r = fr // ny
    vmem = pl.BlockSpec(memory_space=pltpu.VMEM)
    hbm = pl.BlockSpec(memory_space=pltpu.HBM)
    dma = pltpu.SemaphoreType.DMA
    filt, gram = pl.pallas_call(
        functools.partial(filter_kernel, nx, ny),
        out_shape=(
            jax.ShapeDtypeStruct((cx, cy, cz, 2 * fr), BF16),
            jax.ShapeDtypeStruct((ny, r, fr), F32),
        ),
        in_specs=[hbm, hbm],
        out_specs=(vmem, vmem),
        scratch_shapes=[
            pltpu.VMEM((cx, cy, cz, fr), BF16),
            pltpu.VMEM((cx, cy, cz), jnp.int32),
            dma((2,)),
            pltpu.VMEM((cx, RAD, cz, fr), BF16),
            pltpu.VMEM((cx, RAD, cz, fr), BF16),
            pltpu.VMEM((cx, cy, cz, fr), BF16),
            pltpu.VMEM((RAD, cy, cz, fr), BF16),
            pltpu.VMEM((RAD, cy, cz, fr), BF16),
            pltpu.VMEM((cx + 2 * RAD, cy, cz, fr), F32),
            pltpu.VMEM((cy, cz, fr), F32),
            pltpu.VMEM((cz, 3 * cz), BF16),
            pltpu.VMEM((cz, cx * cy), BF16),
            pltpu.VMEM((fr, 2 * fr), F32),
            pltpu.VMEM((ny, r, fr), F32),
            pltpu.VMEM((ny, r, fr), F32),
            pltpu.VMEM((nx, r, fr), F32),
            pltpu.VMEM((ny, r, fr), F32),
            dma((cx,)), dma((cx,)), dma((cx,)), dma((cx,)),
            dma((RAD,)), dma((RAD,)), dma((RAD,)), dma((RAD,)),
            dma((ny,)), dma((ny,)), dma((nx,)), dma((nx,)), dma((ny,)), dma((ny,)),
        ],
        compiler_params=pltpu.CompilerParams(
            collective_id=0, has_side_effects=True, vmem_limit_bytes=28 * 1024 * 1024),
    )(movie, brain_mask)
    gram = gram.reshape(fr, fr)
    fitted, propagator = pl.pallas_call(
        fit_kernel,
        grid=(cx,),
        out_shape=(
            jax.ShapeDtypeStruct((cx, cy, cz, fr), BF16),
            jax.ShapeDtypeStruct((fr - 1, fr - 1), F32),
        ),
        in_specs=[
            pl.BlockSpec((fr, fr), lambda i: (0, 0)),
            vmem,
        ],
        out_specs=(
            pl.BlockSpec((1, cy, cz, fr), lambda i: (i, 0, 0, 0)),
            pl.BlockSpec((fr - 1, fr - 1), lambda i: (0, 0)),
        ),
        scratch_shapes=[
            pltpu.VMEM((fr, fr), F32),
            pltpu.VMEM((2 * fr, 2 * fr), BF16),
            pltpu.VMEM((BLK, BLK, fr), F32),
            pltpu.VMEM((BLK, fr), F32),
        ],
        compiler_params=pltpu.CompilerParams(vmem_limit_bytes=16 * 1024 * 1024),
    )(gram, filt)
    return fitted, propagator


def solution(mesh):
    nx, ny = mesh.shape["gx"], mesh.shape["gy"]
    return jax.shard_map(
        functools.partial(on_device, nx, ny),
        mesh=mesh,
        in_specs=(P("gx", "gy", None, None), P("gx", "gy", None)),
        out_specs=(P("gx", "gy", None, None), P()),
        check_vma=False,
    )
```

```python
import functools

import numpy as np
import jax
import jax.numpy as jnp
from jax import lax
from jax.experimental import pallas as pl
from jax.experimental.pallas import tpu as pltpu
from jax.sharding import PartitionSpec as P

RAD = 4
MESH = pl.DeviceIdType.MESH
F32 = jnp.float32
BF16 = jnp.bfloat16


def weights():
    k = np.arange(-RAD, RAD + 1).astype(np.float32)
    sigma = RAD / 2.0
    raw = np.exp(-k * k / np.float32(2.0 * sigma * sigma)).astype(np.float32)
    w = raw / raw.sum(dtype=np.float32)
    return [float(w[RAD + j]) for j in range(RAD + 1)]


W = weights()


def blur9(items, at):
    total = W[0] * items[at + RAD]
    for k in range(1, RAD + 1):
        total = total + W[k] * (items[at + RAD - k] + items[at + RAD + k])
    return total


def split(v):
    hi = v.astype(BF16)
    return hi, (v - hi.astype(F32)).astype(BF16)


def filter_kernel(
    nx, ny,
    movie_hbm, mask_hbm, filt_hbm, gram_out,
    movie, mask, local, filt, fsem, ylo, yhi, ysend, xlo, xhi, zy, yb, maskx, band, maskt, gacc, gpart, rsbuf, xbuf, gfull,
    ysl, ysh, yrl, yrh, xsl, xsh, xrl, xrh, s1, r1, s2, r2, s3, r3,
):
    cx, cy, cz, fr = movie.shape
    gx, gy = lax.axis_index("gx"), lax.axis_index("gy")
    load_movie = pltpu.make_async_copy(movie_hbm, movie, local.at[0])
    load_mask = pltpu.make_async_copy(mask_hbm, mask, local.at[1])
    load_movie.start()
    load_mask.start()
    barrier = pltpu.get_barrier_semaphore()

    def hello_y(d, c):
        pl.semaphore_signal(barrier, inc=1, device_id=(gx, lax.rem(gy + d, ny)), device_id_type=MESH)
        return c

    def hello_x(d, c):
        pl.semaphore_signal(barrier, inc=1, device_id=(lax.rem(gx + d, nx), gy), device_id_type=MESH)
        return c

    lax.fori_loop(1, ny, hello_y, 0)
    lax.fori_loop(1, nx, hello_x, 0)
    pl.semaphore_wait(barrier, ny - 1 + nx - 1)

    has_yl, has_yh = gy > 0, gy < ny - 1
    has_xl, has_xh = gx > 0, gx < nx - 1

    def order(i):
        return jnp.where(i % 2 == 0, i // 2, cx - 1 - i // 2)

    def y_up(l):
        return pltpu.make_async_remote_copy(
            src_ref=movie_hbm.at[l, pl.ds(cy - RAD, RAD)], dst_ref=ylo.at[l],
            send_sem=ysl.at[l], recv_sem=yrl.at[l],
            device_id=(gx, gy + 1), device_id_type=MESH)

    def y_down(l):
        return pltpu.make_async_remote_copy(
            src_ref=movie_hbm.at[l, pl.ds(0, RAD)], dst_ref=yhi.at[l],
            send_sem=ysh.at[l], recv_sem=yrh.at[l],
            device_id=(gx, gy - 1), device_id_type=MESH)

    def x_up(j):
        return pltpu.make_async_remote_copy(
            src_ref=ysend.at[cx - RAD + j], dst_ref=xlo.at[j],
            send_sem=xsl.at[j], recv_sem=xrl.at[j],
            device_id=(gx + 1, gy), device_id_type=MESH)

    def x_down(j):
        return pltpu.make_async_remote_copy(
            src_ref=ysend.at[j], dst_ref=xhi.at[j],
            send_sem=xsh.at[j], recv_sem=xrh.at[j],
            device_id=(gx - 1, gy), device_id_type=MESH)

    def start_y(i, c):
        l = order(i)

        @pl.when(has_yh)
        def _():
            y_up(l).start()

        @pl.when(has_yl)
        def _():
            y_down(l).start()
        return c

    lax.fori_loop(0, cx, start_y, 0)

    @pl.when(jnp.logical_not(has_yl))
    def _():
        ylo[...] = jnp.zeros_like(ylo)

    @pl.when(jnp.logical_not(has_yh))
    def _():
        yhi[...] = jnp.zeros_like(yhi)

    @pl.when(jnp.logical_not(has_xl))
    def _():
        xlo[...] = jnp.zeros_like(xlo)

    @pl.when(jnp.logical_not(has_xh))
    def _():
        xhi[...] = jnp.zeros_like(xhi)

    dist = jnp.abs(lax.broadcasted_iota(jnp.int32, (cz, cz), 0) - lax.broadcasted_iota(jnp.int32, (cz, cz), 1))
    t = jnp.zeros((cz, cz), F32)
    for k in range(RAD + 1):
        t = jnp.where(dist == k, W[k], t)
    th, tl = split(t)
    band[:, 0:cz] = th
    band[:, cz:2 * cz] = tl
    band[:, 2 * cz:3 * cz] = th
    load_mask.wait()
    maskt[...] = jnp.transpose(mask[...].astype(F32).reshape(cx * cy, cz)).astype(BF16)
    gacc[...] = jnp.zeros_like(gacc)

    load_movie.wait()
    ZT = 16

    def z_pair(pieces, lhs, to, y):
        v = jnp.dot(lhs, jnp.concatenate(pieces, axis=0), preferred_element_type=F32)
        zy[to, y] = v[:, 0:fr]
        zy[to, y + 1] = v[:, fr:2 * fr]

    def halo_layer(src, j, to):
        for y in range(0, cy, 2):
            h = jnp.concatenate([src[j, y], src[j, y + 1]], axis=1)
            z_pair([h, h], band[:, 0:2 * cz], to, y)

    def halo_step(j):
        @pl.when(has_xl)
        def _():
            x_up(RAD - 1 - j).wait_recv()

        @pl.when(has_xh)
        def _():
            x_down(j).wait_recv()
        halo_layer(xlo, RAD - 1 - j, RAD - 1 - j)
        halo_layer(xhi, j, cx + RAD + j)

    def y_layer(i, c):
        l = order(i)

        @pl.when(has_yl)
        def _():
            y_up(l).wait_recv()

        @pl.when(has_yh)
        def _():
            y_down(l).wait_recv()

        def tile(z, c2):
            rows = pl.ds(pl.multiple_of(z * ZT, ZT), ZT)
            items = [ylo[l, k, rows, :].astype(F32) for k in range(RAD)]
            items += [movie[l, k, rows, :].astype(F32) for k in range(cy)]
            items += [yhi[l, k, rows, :].astype(F32) for k in range(RAD)]
            for y in range(cy):
                v = blur9(items, y)
                yb[y, rows, :] = v
                ysend[l, y, rows, :] = v.astype(BF16)
            return c2

        lax.fori_loop(0, cz // ZT, tile, 0)

        @pl.when(jnp.logical_and(i % 2 == 0, has_xl))
        def _():
            x_down(i // 2).start()

        @pl.when(jnp.logical_and(i % 2 == 1, has_xh))
        def _():
            x_up(RAD - 1 - i // 2).start()

        lanes = lax.broadcasted_iota(jnp.int32, (cx * cy, fr), 0)
        for y in range(0, cy, 2):
            parts = [split(yb[y + k]) for k in range(2)]
            hi = jnp.concatenate([p[0] for p in parts], axis=1)
            lo = jnp.concatenate([p[1] for p in parts], axis=1)
            z_pair([hi, hi, lo], band[...], l + RAD, y)
            for k in range(2):
                one = jnp.where(lanes == l * cy + y + k, 1.0, 0.0).astype(BF16)
                maskx[l, y + k] = jnp.dot(maskt[...], one, preferred_element_type=F32).astype(BF16)

        return c

    lax.fori_loop(0, cx, y_layer, 0)

    def save(l):
        return pltpu.make_async_copy(filt.at[l], filt_hbm.at[l], fsem.at[l])

    def x_layer(l):
        def tile(z, c):
            rows = pl.ds(pl.multiple_of(z * ZT, ZT), ZT)
            for y in range(cy):
                blur = blur9([zy[l + k, y, rows, :] for k in range(2 * RAD + 1)], 0)
                f = maskx[l, y, rows, :].astype(F32) * (movie[l, y, rows, :].astype(F32) - blur)
                fh, fl = split(f)
                filt[l, y, rows, 0:fr] = fh
                filt[l, y, rows, fr:2 * fr] = fl
            return c
        lax.fori_loop(0, cz // ZT, tile, 0)
        save(l).start()
        both = filt[l].reshape(cy * cz, 2 * fr)
        gacc[...] += lax.dot_general(
            both[:, 0:fr], both, (((0,), (0,)), ((), ())), preferred_element_type=F32)

    def x_step(j, c):
        halo_step(j)

        def two(s, c2):
            x_layer(jnp.where(s == 0, RAD - 1 - j, cx - RAD + j))
            return c2
        lax.fori_loop(0, 2, two, 0)
        return c

    lax.fori_loop(0, RAD, x_step, 0)

    g = gacc[:, 0:fr] + gacc[:, fr:2 * fr] + jnp.transpose(gacc[:, fr:2 * fr])
    r = fr // ny
    for p in range(ny):
        gpart[p] = g[p * r:(p + 1) * r]

    def scatter(d):
        to = lax.rem(gy + d, ny)
        return pltpu.make_async_remote_copy(
            src_ref=gpart.at[to], dst_ref=rsbuf.at[d], send_sem=s1.at[d], recv_sem=r1.at[d],
            device_id=(gx, to), device_id_type=MESH)

    def across(d):
        return pltpu.make_async_remote_copy(
            src_ref=xbuf.at[gx], dst_ref=xbuf.at[gx], send_sem=s2.at[d], recv_sem=r2.at[d],
            device_id=(lax.rem(gx + d, nx), gy), device_id_type=MESH)

    def gather(d):
        return pltpu.make_async_remote_copy(
            src_ref=gfull.at[gy], dst_ref=gfull.at[gy], send_sem=s3.at[d], recv_sem=r3.at[d],
            device_id=(gx, lax.rem(gy + d, ny)), device_id_type=MESH)

    def each(n, f):
        def body(d, c):
            f(d)
            return c
        lax.fori_loop(1, n, body, 0)

    each(ny, lambda d: scatter(d).start())
    each(ny, lambda d: scatter(d).wait_recv())
    total = gpart[gy]
    for d in range(1, ny):
        total = total + rsbuf[d]
    xbuf[gx] = total
    each(nx, lambda d: across(d).start())
    each(nx, lambda d: across(d).wait_recv())
    total = xbuf[0]
    for d in range(1, nx):
        total = total + xbuf[d]
    gfull[gy] = total
    each(ny, lambda d: gather(d).start())
    each(ny, lambda d: gather(d).wait_recv())
    gram_out[...] = gfull[...]

    each(ny, lambda d: scatter(d).wait_send())
    each(nx, lambda d: across(d).wait_send())
    each(ny, lambda d: gather(d).wait_send())

    def drain_y(l, c):
        @pl.when(has_yh)
        def _():
            y_up(l).wait_send()

        @pl.when(has_yl)
        def _():
            y_down(l).wait_send()
        return c

    def drain_x(j, c):
        @pl.when(has_xh)
        def _():
            x_up(j).wait_send()

        @pl.when(has_xl)
        def _():
            x_down(j).wait_send()
        return c

    def drain_f(l, c):
        save(l).wait()
        return c

    lax.fori_loop(0, cx, drain_f, 0)
    lax.fori_loop(0, cx, drain_y, 0)
    lax.fori_loop(0, RAD, drain_x, 0)


BLK = 8


def sweep_block(a, dbuf, zbuf, start):
    n = a.shape[0]
    row = lax.broadcasted_iota(jnp.int32, (n, n), 1)
    lane = lax.broadcasted_iota(jnp.int32, (BLK, n), 1)
    sub = lax.broadcasted_iota(jnp.int32, (BLK, n), 0)
    inside = (lane >= start) & (lane < start + BLK)
    panel = a[start:start + BLK, :]
    u = jnp.where(inside, 0.0, panel)
    zbuf[...] = jnp.where(lane == start + sub, -1.0, u)
    for j in range(BLK):
        dbuf[j] = jnp.broadcast_to(panel[:, start + j:start + j + 1], (BLK, n))
    d = {(i, j): jnp.broadcast_to(dbuf[j, i:i + 1, :], (BLK, n)) for j in range(BLK) for i in range(j + 1)}
    z = [jnp.broadcast_to(zbuf[i:i + 1, :], (BLK, n)) for i in range(BLK)]
    inverses, multipliers = {}, {}
    for s in range(0, BLK, 2):
        p, q, r = d[s, s], d[s, s + 1], d[s + 1, s + 1]
        inv = 1.0 / (p * r - q * q)
        ip, iq, ir = r * inv, -(q * inv), p * inv
        inverses[s] = (ip, iq, ir)
        for i in range(s + 2, BLK):
            m0 = d[s, i] * ip + d[s + 1, i] * iq
            m1 = d[s, i] * iq + d[s + 1, i] * ir
            multipliers[s, i] = (m0, m1)
            for j in range(i, BLK):
                d[i, j] = d[i, j] - (m0 * d[s, j] + m1 * d[s + 1, j])
            z[i] = z[i] - (m0 * z[s] + m1 * z[s + 1])
    for s in range(BLK - 2, -1, -2):
        ip, iq, ir = inverses[s]
        w0, w1 = ip * z[s] + iq * z[s + 1], iq * z[s] + ir * z[s + 1]
        for i in range(BLK - 1, s + 1, -1):
            m0, m1 = multipliers[s, i]
            w0, w1 = w0 - m0 * z[i], w1 - m1 * z[i]
        z[s], z[s + 1] = w0, w1
    full = z[0]
    for i in range(1, BLK):
        full = jnp.where(sub == i, z[i], full)
    update = lax.dot_general(
        u, full, (((0,), (0,)), ((), ())), precision=lax.Precision.HIGHEST, preferred_element_type=F32)
    a[...] = jnp.where((row >= start) & (row < start + BLK), 0.0, a[...]) - update
    a[start:start + BLK, :] = full


def fit_kernel(gram, filt_hbm, out_hbm, prop, a, m, dbuf, zbuf, filt, out, isem, osem):
    fr = gram.shape[0]
    load = pltpu.make_async_copy(filt_hbm, filt, isem.at[0])
    load.start()

    g = gram[...]
    row = lax.broadcasted_iota(jnp.int32, (fr, fr), 0)
    col = lax.broadcasted_iota(jnp.int32, (fr, fr), 1)
    diag = jnp.where((row == col) & (row < fr - 1), g, 0.0)
    lam = 0.5 * jnp.sum(diag) / (fr - 1)
    scaled = g / lam
    last = (row == fr - 1) | (col == fr - 1)
    a[...] = jnp.where(last, 0.0, scaled) + jnp.where(row == col, 1.0, 0.0)
    for start in range(0, fr, BLK):
        sweep_block(a, dbuf, zbuf, start)
    x = -jnp.dot(a[...], jnp.where(row == fr - 1, 0.0, scaled),
                 precision=lax.Precision.HIGHEST, preferred_element_type=F32)
    prop[...] = x[0:fr - 1, 1:fr]
    adv = jnp.where(col == 0, jnp.where(row == 0, 1.0, 0.0), x)
    mh, ml = split(adv)
    m[0:fr, 0:fr] = mh
    m[0:fr, fr:2 * fr] = ml
    m[fr:2 * fr, 0:fr] = mh
    m[fr:2 * fr, fr:2 * fr] = jnp.zeros((fr, fr), BF16)

    load.wait()

    def save(i):
        return pltpu.make_async_copy(out.at[i], out_hbm.at[i], osem.at[i])

    def layer(i, c):
        for y in range(filt.shape[1]):
            v = jnp.dot(filt[i, y], m[...], preferred_element_type=F32)
            out[i, y] = (v[:, 0:fr] + v[:, fr:2 * fr]).astype(BF16)
        save(i).start()
        return c

    def drain(i, c):
        save(i).wait()
        return c

    lax.fori_loop(0, filt.shape[0], layer, 0)
    lax.fori_loop(0, filt.shape[0], drain, 0)


def on_device(nx, ny, movie, brain_mask):
    cx, cy, cz, fr = movie.shape
    r = fr // ny
    vmem = pl.BlockSpec(memory_space=pltpu.VMEM)
    hbm = pl.BlockSpec(memory_space=pltpu.HBM)
    dma = pltpu.SemaphoreType.DMA
    filt, gram = pl.pallas_call(
        functools.partial(filter_kernel, nx, ny),
        out_shape=(
            jax.ShapeDtypeStruct((cx, cy, cz, 2 * fr), BF16),
            jax.ShapeDtypeStruct((ny, r, fr), F32),
        ),
        in_specs=[hbm, hbm],
        out_specs=(hbm, vmem),
        scratch_shapes=[
            pltpu.VMEM((cx, cy, cz, fr), BF16),
            pltpu.VMEM((cx, cy, cz), jnp.int32),
            dma((2,)),
            pltpu.VMEM((cx, cy, cz, 2 * fr), BF16),
            dma((cx,)),
            pltpu.VMEM((cx, RAD, cz, fr), BF16),
            pltpu.VMEM((cx, RAD, cz, fr), BF16),
            pltpu.VMEM((cx, cy, cz, fr), BF16),
            pltpu.VMEM((RAD, cy, cz, fr), BF16),
            pltpu.VMEM((RAD, cy, cz, fr), BF16),
            pltpu.VMEM((cx + 2 * RAD, cy, cz, fr), F32),
            pltpu.VMEM((cy, cz, fr), F32),
            pltpu.VMEM((cx, cy, cz, fr), BF16),
            pltpu.VMEM((cz, 3 * cz), BF16),
            pltpu.VMEM((cz, cx * cy), BF16),
            pltpu.VMEM((fr, 2 * fr), F32),
            pltpu.VMEM((ny, r, fr), F32),
            pltpu.VMEM((ny, r, fr), F32),
            pltpu.VMEM((nx, r, fr), F32),
            pltpu.VMEM((ny, r, fr), F32),
            dma((cx,)), dma((cx,)), dma((cx,)), dma((cx,)),
            dma((RAD,)), dma((RAD,)), dma((RAD,)), dma((RAD,)),
            dma((ny,)), dma((ny,)), dma((nx,)), dma((nx,)), dma((ny,)), dma((ny,)),
        ],
        compiler_params=pltpu.CompilerParams(
            collective_id=0, has_side_effects=True, vmem_limit_bytes=60 * 1024 * 1024),
    )(movie, brain_mask)
    gram = gram.reshape(fr, fr)
    fitted, propagator = pl.pallas_call(
        fit_kernel,
        out_shape=(
            jax.ShapeDtypeStruct((cx, cy, cz, fr), BF16),
            jax.ShapeDtypeStruct((fr - 1, fr - 1), F32),
        ),
        in_specs=[vmem, hbm],
        out_specs=(hbm, vmem),
        scratch_shapes=[
            pltpu.VMEM((fr, fr), F32),
            pltpu.VMEM((2 * fr, 2 * fr), BF16),
            pltpu.VMEM((BLK, BLK, fr), F32),
            pltpu.VMEM((BLK, fr), F32),
            pltpu.VMEM((cx, cy, cz, 2 * fr), BF16),
            pltpu.VMEM((cx, cy, cz, fr), BF16),
            dma((1,)),
            dma((cx,)),
        ],
        compiler_params=pltpu.CompilerParams(vmem_limit_bytes=60 * 1024 * 1024),
    )(gram, filt)
    return fitted, propagator


def solution(mesh):
    nx, ny = mesh.shape["gx"], mesh.shape["gy"]
    return jax.shard_map(
        functools.partial(on_device, nx, ny),
        mesh=mesh,
        in_specs=(P("gx", "gy", None, None), P("gx", "gy", None)),
        out_specs=(P("gx", "gy", None, None), P()),
        check_vma=False,
    )
```

```python
import functools

import numpy as np
import jax
import jax.numpy as jnp
from jax import lax
from jax.experimental import pallas as pl
from jax.experimental.pallas import tpu as pltpu
from jax.sharding import PartitionSpec as P

RAD = 4
AHEAD = 3
MESH = pl.DeviceIdType.MESH
F32 = jnp.float32
BF16 = jnp.bfloat16


def weights():
    k = np.arange(-RAD, RAD + 1).astype(np.float32)
    sigma = RAD / 2.0
    raw = np.exp(-k * k / np.float32(2.0 * sigma * sigma)).astype(np.float32)
    w = raw / raw.sum(dtype=np.float32)
    return [float(w[RAD + j]) for j in range(RAD + 1)]


W = weights()


def blur9(items, at):
    total = W[0] * items[at + RAD]
    for k in range(1, RAD + 1):
        total = total + W[k] * (items[at + RAD - k] + items[at + RAD + k])
    return total


def split(v):
    hi = v.astype(BF16)
    return hi, (v - hi.astype(F32)).astype(BF16)


def filter_kernel(
    nx, ny,
    movie_hbm, mask_hbm, filt_hbm, gram_out,
    movie, mask, local, filt, fsem, xlo, xhi, xsend, ylo, yhi, zy, yb, maskx, band, maskt, gacc, gpart, rsbuf, xbuf, gfull,
    xsl, xsh, xrl, xrh, ysl, ysh, yrl, yrh, s1, r1, s2, r2, s3, r3,
):
    cx, cy, cz, fr = movie.shape
    gx, gy = lax.axis_index("gx"), lax.axis_index("gy")
    load_movie = pltpu.make_async_copy(movie_hbm, movie, local.at[0])
    load_mask = pltpu.make_async_copy(mask_hbm, mask, local.at[1])
    load_movie.start()
    load_mask.start()
    barrier = pltpu.get_barrier_semaphore()

    def hello_y(d, c):
        pl.semaphore_signal(barrier, inc=1, device_id=(gx, lax.rem(gy + d, ny)), device_id_type=MESH)
        return c

    def hello_x(d, c):
        pl.semaphore_signal(barrier, inc=1, device_id=(lax.rem(gx + d, nx), gy), device_id_type=MESH)
        return c

    lax.fori_loop(1, ny, hello_y, 0)
    lax.fori_loop(1, nx, hello_x, 0)
    pl.semaphore_wait(barrier, ny - 1 + nx - 1)

    has_yl, has_yh = gy > 0, gy < ny - 1
    has_xl, has_xh = gx > 0, gx < nx - 1

    def order(i):
        return jnp.where(i % 2 == 0, i // 2, cy - 1 - i // 2)

    def x_up(c):
        return pltpu.make_async_remote_copy(
            src_ref=movie_hbm.at[pl.ds(cx - RAD, RAD), c], dst_ref=xlo.at[c],
            send_sem=xsl.at[c], recv_sem=xrl.at[c],
            device_id=(gx + 1, gy), device_id_type=MESH)

    def x_down(c):
        return pltpu.make_async_remote_copy(
            src_ref=movie_hbm.at[pl.ds(0, RAD), c], dst_ref=xhi.at[c],
            send_sem=xsh.at[c], recv_sem=xrh.at[c],
            device_id=(gx - 1, gy), device_id_type=MESH)

    def y_up(j):
        return pltpu.make_async_remote_copy(
            src_ref=xsend.at[cy - RAD + j], dst_ref=ylo.at[j],
            send_sem=ysl.at[j], recv_sem=yrl.at[j],
            device_id=(gx, gy + 1), device_id_type=MESH)

    def y_down(j):
        return pltpu.make_async_remote_copy(
            src_ref=xsend.at[j], dst_ref=yhi.at[j],
            send_sem=ysh.at[j], recv_sem=yrh.at[j],
            device_id=(gx, gy - 1), device_id_type=MESH)

    def start_x(i, carry):
        c = order(i)

        @pl.when(has_xh)
        def _():
            x_up(c).start()

        @pl.when(has_xl)
        def _():
            x_down(c).start()
        return carry

    lax.fori_loop(0, AHEAD, start_x, 0)

    @pl.when(jnp.logical_not(has_yl))
    def _():
        ylo[...] = jnp.zeros_like(ylo)

    @pl.when(jnp.logical_not(has_yh))
    def _():
        yhi[...] = jnp.zeros_like(yhi)

    @pl.when(jnp.logical_not(has_xl))
    def _():
        xlo[...] = jnp.zeros_like(xlo)

    @pl.when(jnp.logical_not(has_xh))
    def _():
        xhi[...] = jnp.zeros_like(xhi)

    dist = jnp.abs(lax.broadcasted_iota(jnp.int32, (cz, cz), 0) - lax.broadcasted_iota(jnp.int32, (cz, cz), 1))
    t = jnp.zeros((cz, cz), F32)
    for k in range(RAD + 1):
        t = jnp.where(dist == k, W[k], t)
    th, tl = split(t)
    band[:, 0:cz] = th
    band[:, cz:2 * cz] = tl
    band[:, 2 * cz:3 * cz] = th
    load_mask.wait()
    maskt[...] = jnp.transpose(mask[...].astype(F32).reshape(cx * cy, cz)).astype(BF16)
    gacc[...] = jnp.zeros_like(gacc)

    load_movie.wait()
    ZT = 16

    def z_pair(pieces, lhs, to, y):
        v = jnp.dot(lhs, jnp.concatenate(pieces, axis=0), preferred_element_type=F32)
        zy[to, y] = v[:, 0:fr]
        zy[to, y + 1] = v[:, fr:2 * fr]

    def halo_column(src, j, to):
        for x in range(0, cx, 2):
            h = jnp.concatenate([src[j, x], src[j, x + 1]], axis=1)
            z_pair([h, h], band[:, 0:2 * cz], to, x)

    def x_column(i, carry):
        c = order(i)

        @pl.when(has_xl)
        def _():
            x_up(c).wait_recv()

        @pl.when(has_xh)
        def _():
            x_down(c).wait_recv()

        @pl.when(i + AHEAD < cy)
        def _():
            start_x(i + AHEAD, 0)

        def tile(z, c2):
            rows = pl.ds(pl.multiple_of(z * ZT, ZT), ZT)
            items = [xlo[c, k, rows, :].astype(F32) for k in range(RAD)]
            items += [movie[k, c, rows, :].astype(F32) for k in range(cx)]
            items += [xhi[c, k, rows, :].astype(F32) for k in range(RAD)]
            for x in range(cx):
                v = blur9(items, x)
                yb[x, rows, :] = v
                xsend[c, x, rows, :] = v.astype(BF16)
            return c2

        lax.fori_loop(0, cz // ZT, tile, 0)

        @pl.when(jnp.logical_and(i % 2 == 0, has_yl))
        def _():
            y_down(i // 2).start()

        @pl.when(jnp.logical_and(i % 2 == 1, has_yh))
        def _():
            y_up(RAD - 1 - i // 2).start()

        lanes = lax.broadcasted_iota(jnp.int32, (cx * cy, fr), 0)
        for x in range(0, cx, 2):
            parts = [split(yb[x + k]) for k in range(2)]
            hi = jnp.concatenate([p[0] for p in parts], axis=1)
            lo = jnp.concatenate([p[1] for p in parts], axis=1)
            z_pair([hi, hi, lo], band[...], c + RAD, x)
            for k in range(2):
                one = jnp.where(lanes == (x + k) * cy + c, 1.0, 0.0).astype(BF16)
                maskx[c, x + k] = jnp.dot(maskt[...], one, preferred_element_type=F32).astype(BF16)
        return carry

    lax.fori_loop(0, cy, x_column, 0)

    def save(c):
        return pltpu.make_async_copy(filt.at[c], filt_hbm.at[c], fsem.at[c])

    def y_column(c):
        def tile(z, carry):
            rows = pl.ds(pl.multiple_of(z * ZT, ZT), ZT)
            for x in range(cx):
                blur = blur9([zy[c + k, x, rows, :] for k in range(2 * RAD + 1)], 0)
                f = maskx[c, x, rows, :].astype(F32) * (movie[x, c, rows, :].astype(F32) - blur)
                fh, fl = split(f)
                filt[c, x, rows, 0:fr] = fh
                filt[c, x, rows, fr:2 * fr] = fl
            return carry
        lax.fori_loop(0, cz // ZT, tile, 0)
        save(c).start()
        both = filt[c].reshape(cx * cz, 2 * fr)
        gacc[...] += lax.dot_general(
            both[:, 0:fr], both, (((0,), (0,)), ((), ())), preferred_element_type=F32)

    def y_step(j, carry):
        @pl.when(has_yl)
        def _():
            y_up(RAD - 1 - j).wait_recv()

        @pl.when(has_yh)
        def _():
            y_down(j).wait_recv()
        halo_column(ylo, RAD - 1 - j, RAD - 1 - j)
        halo_column(yhi, j, cy + RAD + j)

        def two(s, c2):
            y_column(jnp.where(s == 0, RAD - 1 - j, cy - RAD + j))
            return c2
        lax.fori_loop(0, 2, two, 0)
        return carry

    lax.fori_loop(0, RAD, y_step, 0)

    g = gacc[:, 0:fr] + gacc[:, fr:2 * fr] + jnp.transpose(gacc[:, fr:2 * fr])
    r = fr // ny
    for p in range(ny):
        gpart[p] = g[p * r:(p + 1) * r]

    def scatter(d):
        to = lax.rem(gy + d, ny)
        return pltpu.make_async_remote_copy(
            src_ref=gpart.at[to], dst_ref=rsbuf.at[d], send_sem=s1.at[d], recv_sem=r1.at[d],
            device_id=(gx, to), device_id_type=MESH)

    def across(d):
        return pltpu.make_async_remote_copy(
            src_ref=xbuf.at[gx], dst_ref=xbuf.at[gx], send_sem=s2.at[d], recv_sem=r2.at[d],
            device_id=(lax.rem(gx + d, nx), gy), device_id_type=MESH)

    def gather(d):
        return pltpu.make_async_remote_copy(
            src_ref=gfull.at[gy], dst_ref=gfull.at[gy], send_sem=s3.at[d], recv_sem=r3.at[d],
            device_id=(gx, lax.rem(gy + d, ny)), device_id_type=MESH)

    def each(n, f):
        def body(d, c):
            f(d)
            return c
        lax.fori_loop(1, n, body, 0)

    each(ny, lambda d: scatter(d).start())
    each(ny, lambda d: scatter(d).wait_recv())
    total = gpart[gy]
    for d in range(1, ny):
        total = total + rsbuf[d]
    xbuf[gx] = total
    each(nx, lambda d: across(d).start())
    each(nx, lambda d: across(d).wait_recv())
    total = xbuf[0]
    for d in range(1, nx):
        total = total + xbuf[d]
    gfull[gy] = total
    each(ny, lambda d: gather(d).start())
    each(ny, lambda d: gather(d).wait_recv())
    gram_out[...] = gfull[...]

    each(ny, lambda d: scatter(d).wait_send())
    each(nx, lambda d: across(d).wait_send())
    each(ny, lambda d: gather(d).wait_send())

    def drain_x(c, carry):
        @pl.when(has_xh)
        def _():
            x_up(c).wait_send()

        @pl.when(has_xl)
        def _():
            x_down(c).wait_send()
        return carry

    def drain_y(j, carry):
        @pl.when(has_yh)
        def _():
            y_up(j).wait_send()

        @pl.when(has_yl)
        def _():
            y_down(j).wait_send()
        return carry

    def drain_f(c, carry):
        save(c).wait()
        return carry

    lax.fori_loop(0, cy, drain_f, 0)
    lax.fori_loop(0, cy, drain_x, 0)
    lax.fori_loop(0, RAD, drain_y, 0)


BLK = 8


def pieces(v):
    hi = v.astype(BF16)
    rest = v - hi.astype(F32)
    mid = rest.astype(BF16)
    return hi, mid, (rest - mid.astype(F32)).astype(BF16)


def outer(u, v):
    uh, um, ul = pieces(u)
    vh, vm, vl = pieces(v)
    left = jnp.concatenate([uh, uh, um, uh, ul, um], axis=0)
    right = jnp.concatenate([vh, vm, vh, vl, vh, vm], axis=0)
    return lax.dot_general(left, right, (((0,), (0,)), ((), ())), preferred_element_type=F32)


def stack(rows, sub):
    full = rows[0]
    for i in range(1, BLK):
        full = jnp.where(sub == i, rows[i], full)
    return full


def sweep(a, dbuf, zbuf):
    n = a.shape[0]
    cols = lax.broadcasted_iota(jnp.int32, (n, n), 1)
    lane = lax.broadcasted_iota(jnp.int32, (BLK, n), 1)
    sub = lax.broadcasted_iota(jnp.int32, (BLK, n), 0)
    panel = a[0:BLK, :]
    for start in range(0, n, BLK):
        after = start + BLK
        inside = (lane >= start) & (lane < after)
        u = jnp.where(inside, 0.0, panel)
        zbuf[start // BLK % 2] = jnp.where(lane == start + sub, -1.0, u)
        slot = start // BLK % 2
        for j in range(BLK):
            dbuf[slot, j] = jnp.broadcast_to(panel[:, start + j:start + j + 1], (BLK, n))
        if after < n:
            for j in range(BLK):
                dbuf[slot, BLK + j] = jnp.broadcast_to(panel[:, after + j:after + j + 1], (BLK, n))

        def entry(i, j):
            return jnp.broadcast_to(dbuf[slot, j, i:i + 1, :], (BLK, n))

        d = {(i, j): entry(i, j) for j in range(BLK) for i in range(j + 1)}
        z = [jnp.broadcast_to(zbuf[slot, i:i + 1, :], (BLK, n)) for i in range(BLK)]
        inverses, multipliers = {}, {}
        for s in range(0, BLK, 2):
            p, q, r = d[s, s], d[s, s + 1], d[s + 1, s + 1]
            inv = 1.0 / (p * r - q * q)
            ip, iq, ir = r * inv, -(q * inv), p * inv
            inverses[s] = (ip, iq, ir)
            for i in range(s + 2, BLK):
                m0 = d[s, i] * ip + d[s + 1, i] * iq
                m1 = d[s, i] * iq + d[s + 1, i] * ir
                multipliers[s, i] = (m0, m1)
                for j in range(i, BLK):
                    d[i, j] = d[i, j] - (m0 * d[s, j] + m1 * d[s + 1, j])
                z[i] = z[i] - (m0 * z[s] + m1 * z[s + 1])
        for s in range(BLK - 2, -1, -2):
            ip, iq, ir = inverses[s]
            w0, w1 = ip * z[s] + iq * z[s + 1], iq * z[s] + ir * z[s + 1]
            for i in range(BLK - 1, s + 1, -1):
                m0, m1 = multipliers[s, i]
                w0, w1 = w0 - m0 * z[i], w1 - m1 * z[i]
            z[s], z[s + 1] = w0, w1
        if after < n:
            rows = []
            for i in range(BLK):
                terms = [entry(s, BLK + i) * z[s] for s in range(BLK)]
                while len(terms) > 1:
                    terms = [terms[k] + terms[k + 1] for k in range(0, len(terms), 2)]
                rows.append(terms[0])
            panel = jnp.where(inside, 0.0, a[after:after + BLK, :]) - stack(rows, sub)
        full = stack(z, sub)
        a[...] = jnp.where((cols >= start) & (cols < after), 0.0, a[...]) - outer(u, full)
        a[start:after, :] = full


def fit_kernel(gram, filt_hbm, out_hbm, prop, a, m, dbuf, zbuf, filt, out, isem, osem):
    fr = gram.shape[0]
    load = pltpu.make_async_copy(filt_hbm, filt, isem.at[0])
    load.start()

    g = gram[...]
    row = lax.broadcasted_iota(jnp.int32, (fr, fr), 0)
    col = lax.broadcasted_iota(jnp.int32, (fr, fr), 1)
    diag = jnp.where((row == col) & (row < fr - 1), g, 0.0)
    lam = 0.5 * jnp.sum(diag) / (fr - 1)
    scaled = g / lam
    last = (row == fr - 1) | (col == fr - 1)
    a[...] = jnp.where(last, 0.0, scaled) + jnp.where(row == col, 1.0, 0.0)
    sweep(a, dbuf, zbuf)
    x = -jnp.dot(a[...], jnp.where(row == fr - 1, 0.0, scaled),
                 precision=lax.Precision.HIGHEST, preferred_element_type=F32)
    prop[...] = x[0:fr - 1, 1:fr]
    adv = jnp.where(col == 0, jnp.where(row == 0, 1.0, 0.0), x)
    mh, ml = split(adv)
    m[0:fr, 0:fr] = mh
    m[0:fr, fr:2 * fr] = ml
    m[fr:2 * fr, 0:fr] = mh
    m[fr:2 * fr, fr:2 * fr] = jnp.zeros((fr, fr), BF16)

    load.wait()

    def save(i):
        return pltpu.make_async_copy(out.at[i], out_hbm.at[i], osem.at[i])

    def layer(i, c):
        for y in range(out.shape[1]):
            v = jnp.dot(filt[y, i], m[...], preferred_element_type=F32)
            out[i, y] = (v[:, 0:fr] + v[:, fr:2 * fr]).astype(BF16)
        save(i).start()
        return c

    def drain(i, c):
        save(i).wait()
        return c

    lax.fori_loop(0, out.shape[0], layer, 0)
    lax.fori_loop(0, out.shape[0], drain, 0)


def on_device(nx, ny, movie, brain_mask):
    cx, cy, cz, fr = movie.shape
    r = fr // ny
    vmem = pl.BlockSpec(memory_space=pltpu.VMEM)
    hbm = pl.BlockSpec(memory_space=pltpu.HBM)
    dma = pltpu.SemaphoreType.DMA
    filt, gram = pl.pallas_call(
        functools.partial(filter_kernel, nx, ny),
        out_shape=(
            jax.ShapeDtypeStruct((cy, cx, cz, 2 * fr), BF16),
            jax.ShapeDtypeStruct((ny, r, fr), F32),
        ),
        in_specs=[hbm, hbm],
        out_specs=(hbm, vmem),
        scratch_shapes=[
            pltpu.VMEM((cx, cy, cz, fr), BF16),
            pltpu.VMEM((cx, cy, cz), jnp.int32),
            dma((2,)),
            pltpu.VMEM((cy, cx, cz, 2 * fr), BF16),
            dma((cy,)),
            pltpu.VMEM((cy, RAD, cz, fr), BF16),
            pltpu.VMEM((cy, RAD, cz, fr), BF16),
            pltpu.VMEM((cy, cx, cz, fr), BF16),
            pltpu.VMEM((RAD, cx, cz, fr), BF16),
            pltpu.VMEM((RAD, cx, cz, fr), BF16),
            pltpu.VMEM((cy + 2 * RAD, cx, cz, fr), F32),
            pltpu.VMEM((cx, cz, fr), F32),
            pltpu.VMEM((cy, cx, cz, fr), BF16),
            pltpu.VMEM((cz, 3 * cz), BF16),
            pltpu.VMEM((cz, cx * cy), BF16),
            pltpu.VMEM((fr, 2 * fr), F32),
            pltpu.VMEM((ny, r, fr), F32),
            pltpu.VMEM((ny, r, fr), F32),
            pltpu.VMEM((nx, r, fr), F32),
            pltpu.VMEM((ny, r, fr), F32),
            dma((cy,)), dma((cy,)), dma((cy,)), dma((cy,)),
            dma((RAD,)), dma((RAD,)), dma((RAD,)), dma((RAD,)),
            dma((ny,)), dma((ny,)), dma((nx,)), dma((nx,)), dma((ny,)), dma((ny,)),
        ],
        compiler_params=pltpu.CompilerParams(
            collective_id=0, has_side_effects=True, vmem_limit_bytes=60 * 1024 * 1024),
    )(movie, brain_mask)
    gram = gram.reshape(fr, fr)
    fitted, propagator = pl.pallas_call(
        fit_kernel,
        out_shape=(
            jax.ShapeDtypeStruct((cx, cy, cz, fr), BF16),
            jax.ShapeDtypeStruct((fr - 1, fr - 1), F32),
        ),
        in_specs=[vmem, hbm],
        out_specs=(hbm, vmem),
        scratch_shapes=[
            pltpu.VMEM((fr, fr), F32),
            pltpu.VMEM((2 * fr, 2 * fr), BF16),
            pltpu.VMEM((2, 2 * BLK, BLK, fr), F32),
            pltpu.VMEM((2, BLK, fr), F32),
            pltpu.VMEM((cy, cx, cz, 2 * fr), BF16),
            pltpu.VMEM((cx, cy, cz, fr), BF16),
            dma((1,)),
            dma((cx,)),
        ],
        compiler_params=pltpu.CompilerParams(vmem_limit_bytes=60 * 1024 * 1024),
    )(gram, filt)
    return fitted, propagator


def solution(mesh):
    nx, ny = mesh.shape["gx"], mesh.shape["gy"]
    return jax.shard_map(
        functools.partial(on_device, nx, ny),
        mesh=mesh,
        in_specs=(P("gx", "gy", None, None), P("gx", "gy", None)),
        out_specs=(P("gx", "gy", None, None), P()),
        check_vma=False,
    )
```

```python
import functools

import numpy as np
import jax
import jax.numpy as jnp
from jax import lax
from jax.experimental import pallas as pl
from jax.experimental.pallas import tpu as pltpu
from jax.sharding import PartitionSpec as P

RAD = 4
AHEAD = 3
MESH = pl.DeviceIdType.MESH
F32 = jnp.float32
BF16 = jnp.bfloat16


def weights():
    k = np.arange(-RAD, RAD + 1).astype(np.float32)
    sigma = RAD / 2.0
    raw = np.exp(-k * k / np.float32(2.0 * sigma * sigma)).astype(np.float32)
    w = raw / raw.sum(dtype=np.float32)
    return [float(w[RAD + j]) for j in range(RAD + 1)]


W = weights()


def blur9(items, at):
    total = W[0] * items[at + RAD]
    for k in range(1, RAD + 1):
        total = total + W[k] * (items[at + RAD - k] + items[at + RAD + k])
    return total


def split(v):
    hi = v.astype(BF16)
    return hi, (v - hi.astype(F32)).astype(BF16)


def filter_kernel(
    nx, ny,
    movie_hbm, mask_hbm, filt_hbm, gram_out,
    movie, mask, local, filt, fsem, xlo, xhi, xsend, ylo, yhi, zy, yb, maskx, band, maskt, gacc, gpart, rsbuf, xbuf, gfull,
    xsl, xsh, xrl, xrh, ysl, ysh, yrl, yrh, s1, r1, s2, r2, s3, r3,
):
    cx, cy, cz, fr = movie.shape
    gx, gy = lax.axis_index("gx"), lax.axis_index("gy")
    load_movie = pltpu.make_async_copy(movie_hbm, movie, local.at[0])
    load_mask = pltpu.make_async_copy(mask_hbm, mask, local.at[1])
    load_movie.start()
    load_mask.start()
    barrier = pltpu.get_barrier_semaphore()

    def hello_y(d, c):
        pl.semaphore_signal(barrier, inc=1, device_id=(gx, lax.rem(gy + d, ny)), device_id_type=MESH)
        return c

    def hello_x(d, c):
        pl.semaphore_signal(barrier, inc=1, device_id=(lax.rem(gx + d, nx), gy), device_id_type=MESH)
        return c

    lax.fori_loop(1, ny, hello_y, 0)
    lax.fori_loop(1, nx, hello_x, 0)
    pl.semaphore_wait(barrier, ny - 1 + nx - 1)

    has_yl, has_yh = gy > 0, gy < ny - 1
    has_xl, has_xh = gx > 0, gx < nx - 1

    def order(i):
        return jnp.where(i % 2 == 0, i // 2, cy - 1 - i // 2)

    def x_up(c):
        return pltpu.make_async_remote_copy(
            src_ref=movie_hbm.at[pl.ds(cx - RAD, RAD), c], dst_ref=xlo.at[c],
            send_sem=xsl.at[c], recv_sem=xrl.at[c],
            device_id=(gx + 1, gy), device_id_type=MESH)

    def x_down(c):
        return pltpu.make_async_remote_copy(
            src_ref=movie_hbm.at[pl.ds(0, RAD), c], dst_ref=xhi.at[c],
            send_sem=xsh.at[c], recv_sem=xrh.at[c],
            device_id=(gx - 1, gy), device_id_type=MESH)

    def y_up(j):
        return pltpu.make_async_remote_copy(
            src_ref=xsend.at[cy - RAD + j], dst_ref=ylo.at[j],
            send_sem=ysl.at[j], recv_sem=yrl.at[j],
            device_id=(gx, gy + 1), device_id_type=MESH)

    def y_down(j):
        return pltpu.make_async_remote_copy(
            src_ref=xsend.at[j], dst_ref=yhi.at[j],
            send_sem=ysh.at[j], recv_sem=yrh.at[j],
            device_id=(gx, gy - 1), device_id_type=MESH)

    def start_x(i, carry):
        c = order(i)

        @pl.when(has_xh)
        def _():
            x_up(c).start()

        @pl.when(has_xl)
        def _():
            x_down(c).start()
        return carry

    lax.fori_loop(0, AHEAD, start_x, 0)

    @pl.when(jnp.logical_not(has_yl))
    def _():
        ylo[...] = jnp.zeros_like(ylo)

    @pl.when(jnp.logical_not(has_yh))
    def _():
        yhi[...] = jnp.zeros_like(yhi)

    @pl.when(jnp.logical_not(has_xl))
    def _():
        xlo[...] = jnp.zeros_like(xlo)

    @pl.when(jnp.logical_not(has_xh))
    def _():
        xhi[...] = jnp.zeros_like(xhi)

    dist = jnp.abs(lax.broadcasted_iota(jnp.int32, (cz, cz), 0) - lax.broadcasted_iota(jnp.int32, (cz, cz), 1))
    t = jnp.zeros((cz, cz), F32)
    for k in range(RAD + 1):
        t = jnp.where(dist == k, W[k], t)
    th, tl = split(t)
    band[:, 0:cz] = th
    band[:, cz:2 * cz] = tl
    band[:, 2 * cz:3 * cz] = th
    load_mask.wait()
    maskt[...] = jnp.transpose(mask[...].astype(F32).reshape(cx * cy, cz)).astype(BF16)
    gacc[...] = jnp.zeros_like(gacc)

    load_movie.wait()
    ZT = 16

    def z_pair(pieces, lhs, to, y):
        v = jnp.dot(lhs, jnp.concatenate(pieces, axis=0), preferred_element_type=F32)
        zy[to, y] = v[:, 0:fr]
        zy[to, y + 1] = v[:, fr:2 * fr]

    def halo_column(src, j, to):
        for x in range(0, cx, 2):
            h = jnp.concatenate([src[j, x], src[j, x + 1]], axis=1)
            z_pair([h, h], band[:, 0:2 * cz], to, x)

    def take_halo(j):
        @pl.when(has_yl)
        def _():
            y_up(RAD - 1 - j).wait_recv()

        @pl.when(has_yh)
        def _():
            y_down(j).wait_recv()
        halo_column(ylo, RAD - 1 - j, RAD - 1 - j)
        halo_column(yhi, j, cy + RAD + j)

    early = 2

    def x_column(i, carry):
        c = order(i)

        @pl.when(has_xl)
        def _():
            x_up(c).wait_recv()

        @pl.when(has_xh)
        def _():
            x_down(c).wait_recv()

        @pl.when(i + AHEAD < cy)
        def _():
            start_x(i + AHEAD, 0)

        def tile(z, c2):
            rows = pl.ds(pl.multiple_of(z * ZT, ZT), ZT)
            items = [xlo[c, k, rows, :].astype(F32) for k in range(RAD)]
            items += [movie[k, c, rows, :].astype(F32) for k in range(cx)]
            items += [xhi[c, k, rows, :].astype(F32) for k in range(RAD)]
            for x in range(cx):
                v = blur9(items, x)
                yb[x, rows, :] = v
                xsend[c, x, rows, :] = v.astype(BF16)
            return c2

        lax.fori_loop(0, cz // ZT, tile, 0)

        @pl.when(jnp.logical_and(i % 2 == 0, has_yl))
        def _():
            y_down(i // 2).start()

        @pl.when(jnp.logical_and(i % 2 == 1, has_yh))
        def _():
            y_up(RAD - 1 - i // 2).start()

        lanes = lax.broadcasted_iota(jnp.int32, (cx * cy, fr), 0)
        for x in range(0, cx, 2):
            parts = [split(yb[x + k]) for k in range(2)]
            hi = jnp.concatenate([p[0] for p in parts], axis=1)
            lo = jnp.concatenate([p[1] for p in parts], axis=1)
            z_pair([hi, hi, lo], band[...], c + RAD, x)
            for k in range(2):
                one = jnp.where(lanes == (x + k) * cy + c, 1.0, 0.0).astype(BF16)
                maskx[c, x + k] = jnp.dot(maskt[...], one, preferred_element_type=F32).astype(BF16)

        @pl.when(jnp.logical_and(i >= 5, i < 5 + early))
        def _():
            take_halo(i - 5)
        return carry

    lax.fori_loop(0, cy, x_column, 0)

    def save(c):
        return pltpu.make_async_copy(filt.at[c], filt_hbm.at[c], fsem.at[c])

    def y_column(c):
        def tile(z, carry):
            rows = pl.ds(pl.multiple_of(z * ZT, ZT), ZT)
            for x in range(cx):
                blur = blur9([zy[c + k, x, rows, :] for k in range(2 * RAD + 1)], 0)
                f = maskx[c, x, rows, :].astype(F32) * (movie[x, c, rows, :].astype(F32) - blur)
                fh, fl = split(f)
                filt[c, x, rows, 0:fr] = fh
                filt[c, x, rows, fr:2 * fr] = fl
            return carry
        lax.fori_loop(0, cz // ZT, tile, 0)
        save(c).start()
        both = filt[c].reshape(cx * cz, 2 * fr)
        gacc[...] += lax.dot_general(
            both[:, 0:fr], both, (((0,), (0,)), ((), ())), preferred_element_type=F32)

    def y_step(j, carry):
        @pl.when(j >= early)
        def _():
            take_halo(j)

        def two(s, c2):
            y_column(jnp.where(s == 0, RAD - 1 - j, cy - RAD + j))
            return c2
        lax.fori_loop(0, 2, two, 0)
        return carry

    lax.fori_loop(0, RAD, y_step, 0)

    g = gacc[:, 0:fr] + gacc[:, fr:2 * fr] + jnp.transpose(gacc[:, fr:2 * fr])
    r = fr // ny
    for p in range(ny):
        gpart[p] = g[p * r:(p + 1) * r]

    def scatter(d):
        to = lax.rem(gy + d, ny)
        return pltpu.make_async_remote_copy(
            src_ref=gpart.at[to], dst_ref=rsbuf.at[d], send_sem=s1.at[d], recv_sem=r1.at[d],
            device_id=(gx, to), device_id_type=MESH)

    def across(d):
        return pltpu.make_async_remote_copy(
            src_ref=xbuf.at[gx], dst_ref=xbuf.at[gx], send_sem=s2.at[d], recv_sem=r2.at[d],
            device_id=(lax.rem(gx + d, nx), gy), device_id_type=MESH)

    def gather(d):
        return pltpu.make_async_remote_copy(
            src_ref=gfull.at[gy], dst_ref=gfull.at[gy], send_sem=s3.at[d], recv_sem=r3.at[d],
            device_id=(gx, lax.rem(gy + d, ny)), device_id_type=MESH)

    def each(n, f):
        def body(d, c):
            f(d)
            return c
        lax.fori_loop(1, n, body, 0)

    each(ny, lambda d: scatter(d).start())
    each(ny, lambda d: scatter(d).wait_recv())
    total = gpart[gy]
    for d in range(1, ny):
        total = total + rsbuf[d]
    xbuf[gx] = total
    each(nx, lambda d: across(d).start())
    each(nx, lambda d: across(d).wait_recv())
    total = xbuf[0]
    for d in range(1, nx):
        total = total + xbuf[d]
    gfull[gy] = total
    each(ny, lambda d: gather(d).start())
    each(ny, lambda d: gather(d).wait_recv())
    gram_out[...] = gfull[...]

    each(ny, lambda d: scatter(d).wait_send())
    each(nx, lambda d: across(d).wait_send())
    each(ny, lambda d: gather(d).wait_send())

    def drain_x(c, carry):
        @pl.when(has_xh)
        def _():
            x_up(c).wait_send()

        @pl.when(has_xl)
        def _():
            x_down(c).wait_send()
        return carry

    def drain_y(j, carry):
        @pl.when(has_yh)
        def _():
            y_up(j).wait_send()

        @pl.when(has_yl)
        def _():
            y_down(j).wait_send()
        return carry

    def drain_f(c, carry):
        save(c).wait()
        return carry

    lax.fori_loop(0, cy, drain_f, 0)
    lax.fori_loop(0, cy, drain_x, 0)
    lax.fori_loop(0, RAD, drain_y, 0)


BLK = 8


def pieces(v):
    hi = v.astype(BF16)
    rest = v - hi.astype(F32)
    mid = rest.astype(BF16)
    return hi, mid, (rest - mid.astype(F32)).astype(BF16)


def outer(u, v):
    uh, um, ul = pieces(u)
    vh, vm, vl = pieces(v)
    left = jnp.concatenate([uh, uh, um, uh, ul, um], axis=0)
    right = jnp.concatenate([vh, vm, vh, vl, vh, vm], axis=0)
    return lax.dot_general(left, right, (((0,), (0,)), ((), ())), preferred_element_type=F32)


def stack(rows, sub):
    full = rows[0]
    for i in range(1, BLK):
        full = jnp.where(sub == i, rows[i], full)
    return full


def sweep(a, dbuf, zbuf):
    n = a.shape[0]
    cols = lax.broadcasted_iota(jnp.int32, (n, n), 1)
    lane = lax.broadcasted_iota(jnp.int32, (BLK, n), 1)
    sub = lax.broadcasted_iota(jnp.int32, (BLK, n), 0)
    panel = a[0:BLK, :]
    for start in range(0, n, BLK):
        after = start + BLK
        inside = (lane >= start) & (lane < after)
        u = jnp.where(inside, 0.0, panel)
        zbuf[start // BLK % 2] = jnp.where(lane == start + sub, -1.0, u)
        slot = start // BLK % 2
        for j in range(BLK):
            dbuf[slot, j] = jnp.broadcast_to(panel[:, start + j:start + j + 1], (BLK, n))
        if after < n:
            for j in range(BLK):
                dbuf[slot, BLK + j] = jnp.broadcast_to(panel[:, after + j:after + j + 1], (BLK, n))

        def entry(i, j):
            return jnp.broadcast_to(dbuf[slot, j, i:i + 1, :], (BLK, n))

        d = {(i, j): entry(i, j) for j in range(BLK) for i in range(j + 1)}
        z = [jnp.broadcast_to(zbuf[slot, i:i + 1, :], (BLK, n)) for i in range(BLK)]
        inverses, multipliers = {}, {}
        for s in range(0, BLK, 2):
            p, q, r = d[s, s], d[s, s + 1], d[s + 1, s + 1]
            inv = 1.0 / (p * r - q * q)
            ip, iq, ir = r * inv, -(q * inv), p * inv
            inverses[s] = (ip, iq, ir)
            for i in range(s + 2, BLK):
                m0 = d[s, i] * ip + d[s + 1, i] * iq
                m1 = d[s, i] * iq + d[s + 1, i] * ir
                multipliers[s, i] = (m0, m1)
                for j in range(i, BLK):
                    d[i, j] = d[i, j] - (m0 * d[s, j] + m1 * d[s + 1, j])
                z[i] = z[i] - (m0 * z[s] + m1 * z[s + 1])
        for s in range(BLK - 2, -1, -2):
            ip, iq, ir = inverses[s]
            w0, w1 = ip * z[s] + iq * z[s + 1], iq * z[s] + ir * z[s + 1]
            for i in range(BLK - 1, s + 1, -1):
                m0, m1 = multipliers[s, i]
                w0, w1 = w0 - m0 * z[i], w1 - m1 * z[i]
            z[s], z[s + 1] = w0, w1
        if after < n:
            rows = []
            for i in range(BLK):
                terms = [entry(s, BLK + i) * z[s] for s in range(BLK)]
                while len(terms) > 1:
                    terms = [terms[k] + terms[k + 1] for k in range(0, len(terms), 2)]
                rows.append(terms[0])
            panel = jnp.where(inside, 0.0, a[after:after + BLK, :]) - stack(rows, sub)
        full = stack(z, sub)
        a[...] = jnp.where((cols >= start) & (cols < after), 0.0, a[...]) - outer(u, full)
        a[start:after, :] = full


def fit_kernel(gram, filt_hbm, out_hbm, prop, a, m, dbuf, zbuf, filt, out, isem, osem):
    fr = gram.shape[0]
    load = pltpu.make_async_copy(filt_hbm, filt, isem.at[0])
    load.start()

    g = gram[...]
    row = lax.broadcasted_iota(jnp.int32, (fr, fr), 0)
    col = lax.broadcasted_iota(jnp.int32, (fr, fr), 1)
    diag = jnp.where((row == col) & (row < fr - 1), g, 0.0)
    lam = 0.5 * jnp.sum(diag) / (fr - 1)
    scaled = g / lam
    last = (row == fr - 1) | (col == fr - 1)
    a[...] = jnp.where(last, 0.0, scaled) + jnp.where(row == col, 1.0, 0.0)
    sweep(a, dbuf, zbuf)
    x = -jnp.dot(a[...], jnp.where(row == fr - 1, 0.0, scaled),
                 precision=lax.Precision.HIGHEST, preferred_element_type=F32)
    prop[...] = x[0:fr - 1, 1:fr]
    adv = jnp.where(col == 0, jnp.where(row == 0, 1.0, 0.0), x)
    mh, ml = split(adv)
    m[0:fr, 0:fr] = mh
    m[0:fr, fr:2 * fr] = ml
    m[fr:2 * fr, 0:fr] = mh
    m[fr:2 * fr, fr:2 * fr] = jnp.zeros((fr, fr), BF16)

    load.wait()

    def save(i):
        return pltpu.make_async_copy(out.at[i], out_hbm.at[i], osem.at[i])

    def layer(i, c):
        for y in range(out.shape[1]):
            v = jnp.dot(filt[y, i], m[...], preferred_element_type=F32)
            out[i, y] = (v[:, 0:fr] + v[:, fr:2 * fr]).astype(BF16)
        save(i).start()
        return c

    def drain(i, c):
        save(i).wait()
        return c

    lax.fori_loop(0, out.shape[0], layer, 0)
    lax.fori_loop(0, out.shape[0], drain, 0)


def on_device(nx, ny, movie, brain_mask):
    cx, cy, cz, fr = movie.shape
    r = fr // ny
    vmem = pl.BlockSpec(memory_space=pltpu.VMEM)
    hbm = pl.BlockSpec(memory_space=pltpu.HBM)
    dma = pltpu.SemaphoreType.DMA
    filt, gram = pl.pallas_call(
        functools.partial(filter_kernel, nx, ny),
        out_shape=(
            jax.ShapeDtypeStruct((cy, cx, cz, 2 * fr), BF16),
            jax.ShapeDtypeStruct((ny, r, fr), F32),
        ),
        in_specs=[hbm, hbm],
        out_specs=(hbm, vmem),
        scratch_shapes=[
            pltpu.VMEM((cx, cy, cz, fr), BF16),
            pltpu.VMEM((cx, cy, cz), jnp.int32),
            dma((2,)),
            pltpu.VMEM((cy, cx, cz, 2 * fr), BF16),
            dma((cy,)),
            pltpu.VMEM((cy, RAD, cz, fr), BF16),
            pltpu.VMEM((cy, RAD, cz, fr), BF16),
            pltpu.VMEM((cy, cx, cz, fr), BF16),
            pltpu.VMEM((RAD, cx, cz, fr), BF16),
            pltpu.VMEM((RAD, cx, cz, fr), BF16),
            pltpu.VMEM((cy + 2 * RAD, cx, cz, fr), F32),
            pltpu.VMEM((cx, cz, fr), F32),
            pltpu.VMEM((cy, cx, cz, fr), BF16),
            pltpu.VMEM((cz, 3 * cz), BF16),
            pltpu.VMEM((cz, cx * cy), BF16),
            pltpu.VMEM((fr, 2 * fr), F32),
            pltpu.VMEM((ny, r, fr), F32),
            pltpu.VMEM((ny, r, fr), F32),
            pltpu.VMEM((nx, r, fr), F32),
            pltpu.VMEM((ny, r, fr), F32),
            dma((cy,)), dma((cy,)), dma((cy,)), dma((cy,)),
            dma((RAD,)), dma((RAD,)), dma((RAD,)), dma((RAD,)),
            dma((ny,)), dma((ny,)), dma((nx,)), dma((nx,)), dma((ny,)), dma((ny,)),
        ],
        compiler_params=pltpu.CompilerParams(
            collective_id=0, has_side_effects=True, vmem_limit_bytes=60 * 1024 * 1024),
    )(movie, brain_mask)
    gram = gram.reshape(fr, fr)
    fitted, propagator = pl.pallas_call(
        fit_kernel,
        out_shape=(
            jax.ShapeDtypeStruct((cx, cy, cz, fr), BF16),
            jax.ShapeDtypeStruct((fr - 1, fr - 1), F32),
        ),
        in_specs=[vmem, hbm],
        out_specs=(hbm, vmem),
        scratch_shapes=[
            pltpu.VMEM((fr, fr), F32),
            pltpu.VMEM((2 * fr, 2 * fr), BF16),
            pltpu.VMEM((2, 2 * BLK, BLK, fr), F32),
            pltpu.VMEM((2, BLK, fr), F32),
            pltpu.VMEM((cy, cx, cz, 2 * fr), BF16),
            pltpu.VMEM((cx, cy, cz, fr), BF16),
            dma((1,)),
            dma((cx,)),
        ],
        compiler_params=pltpu.CompilerParams(vmem_limit_bytes=60 * 1024 * 1024),
    )(gram, filt)
    return fitted, propagator


def solution(mesh):
    nx, ny = mesh.shape["gx"], mesh.shape["gy"]
    return jax.shard_map(
        functools.partial(on_device, nx, ny),
        mesh=mesh,
        in_specs=(P("gx", "gy", None, None), P("gx", "gy", None)),
        out_specs=(P("gx", "gy", None, None), P()),
        check_vma=False,
    )
```

```python
import functools

import numpy as np
import jax
import jax.numpy as jnp
from jax import lax
from jax.experimental import pallas as pl
from jax.experimental.pallas import tpu as pltpu
from jax.sharding import PartitionSpec as P

RAD = 4
AHEAD = 3
MESH = pl.DeviceIdType.MESH
F32 = jnp.float32
BF16 = jnp.bfloat16


def weights():
    k = np.arange(-RAD, RAD + 1).astype(np.float32)
    sigma = RAD / 2.0
    raw = np.exp(-k * k / np.float32(2.0 * sigma * sigma)).astype(np.float32)
    w = raw / raw.sum(dtype=np.float32)
    return [float(w[RAD + j]) for j in range(RAD + 1)]


W = weights()


def blur9(items, at):
    total = W[0] * items[at + RAD]
    for k in range(1, RAD + 1):
        total = total + W[k] * (items[at + RAD - k] + items[at + RAD + k])
    return total


def split(v):
    hi = v.astype(BF16)
    return hi, (v - hi.astype(F32)).astype(BF16)


def filter_kernel(
    nx, ny,
    movie_hbm, mask_hbm, filt_hbm, gram_out,
    movie, mask, local, filt, fsem, xlo, xhi, xsend, ylo, yhi, zy, yb, maskx, band, maskt, gacc, gpart, rsbuf, xbuf, gfull,
    xsl, xsh, xrl, xrh, ysl, ysh, yrl, yrh, s1, r1, s2, r2, s3, r3,
):
    cx, cy, cz, fr = movie.shape
    gx, gy = lax.axis_index("gx"), lax.axis_index("gy")
    load_movie = pltpu.make_async_copy(movie_hbm, movie, local.at[0])
    load_mask = pltpu.make_async_copy(mask_hbm, mask, local.at[1])
    load_movie.start()
    load_mask.start()
    barrier = pltpu.get_barrier_semaphore()

    def hello_y(d, c):
        pl.semaphore_signal(barrier, inc=1, device_id=(gx, lax.rem(gy + d, ny)), device_id_type=MESH)
        return c

    def hello_x(d, c):
        pl.semaphore_signal(barrier, inc=1, device_id=(lax.rem(gx + d, nx), gy), device_id_type=MESH)
        return c

    lax.fori_loop(1, ny, hello_y, 0)
    lax.fori_loop(1, nx, hello_x, 0)
    pl.semaphore_wait(barrier, ny - 1 + nx - 1)

    has_yl, has_yh = gy > 0, gy < ny - 1
    has_xl, has_xh = gx > 0, gx < nx - 1

    def order(i):
        return jnp.where(i % 2 == 0, i // 2, cy - 1 - i // 2)

    def x_up(c):
        return pltpu.make_async_remote_copy(
            src_ref=movie_hbm.at[pl.ds(cx - RAD, RAD), c], dst_ref=xlo.at[c],
            send_sem=xsl.at[c], recv_sem=xrl.at[c],
            device_id=(gx + 1, gy), device_id_type=MESH)

    def x_down(c):
        return pltpu.make_async_remote_copy(
            src_ref=movie_hbm.at[pl.ds(0, RAD), c], dst_ref=xhi.at[c],
            send_sem=xsh.at[c], recv_sem=xrh.at[c],
            device_id=(gx - 1, gy), device_id_type=MESH)

    def y_up(j):
        return pltpu.make_async_remote_copy(
            src_ref=xsend.at[cy - RAD + j], dst_ref=ylo.at[j],
            send_sem=ysl.at[j], recv_sem=yrl.at[j],
            device_id=(gx, gy + 1), device_id_type=MESH)

    def y_down(j):
        return pltpu.make_async_remote_copy(
            src_ref=xsend.at[j], dst_ref=yhi.at[j],
            send_sem=ysh.at[j], recv_sem=yrh.at[j],
            device_id=(gx, gy - 1), device_id_type=MESH)

    def start_x(i, carry):
        c = order(i)

        @pl.when(has_xh)
        def _():
            x_up(c).start()

        @pl.when(has_xl)
        def _():
            x_down(c).start()
        return carry

    lax.fori_loop(0, AHEAD, start_x, 0)

    @pl.when(jnp.logical_not(has_yl))
    def _():
        ylo[...] = jnp.zeros_like(ylo)

    @pl.when(jnp.logical_not(has_yh))
    def _():
        yhi[...] = jnp.zeros_like(yhi)

    @pl.when(jnp.logical_not(has_xl))
    def _():
        xlo[...] = jnp.zeros_like(xlo)

    @pl.when(jnp.logical_not(has_xh))
    def _():
        xhi[...] = jnp.zeros_like(xhi)

    dist = jnp.abs(lax.broadcasted_iota(jnp.int32, (cz, cz), 0) - lax.broadcasted_iota(jnp.int32, (cz, cz), 1))
    t = jnp.zeros((cz, cz), F32)
    for k in range(RAD + 1):
        t = jnp.where(dist == k, W[k], t)
    th, tl = split(t)
    band[:, 0:cz] = th
    band[:, cz:2 * cz] = tl
    band[:, 2 * cz:3 * cz] = th
    load_mask.wait()
    maskt[...] = jnp.transpose(mask[...].astype(F32).reshape(cx * cy, cz)).astype(BF16)
    gacc[...] = jnp.zeros_like(gacc)

    load_movie.wait()
    ZT = 16

    def z_pair(pieces, lhs, to, y):
        v = jnp.dot(lhs, jnp.concatenate(pieces, axis=0), preferred_element_type=F32)
        zy[to, y] = v[:, 0:fr]
        zy[to, y + 1] = v[:, fr:2 * fr]

    def halo_column(src, j, to):
        for x in range(0, cx, 2):
            h = jnp.concatenate([src[j, x], src[j, x + 1]], axis=1)
            z_pair([h, h], band[:, 0:2 * cz], to, x)

    def x_column(i, carry):
        c = order(i)

        @pl.when(has_xl)
        def _():
            x_up(c).wait_recv()

        @pl.when(has_xh)
        def _():
            x_down(c).wait_recv()

        @pl.when(i + AHEAD < cy)
        def _():
            start_x(i + AHEAD, 0)

        def tile(z, c2):
            rows = pl.ds(pl.multiple_of(z * ZT, ZT), ZT)
            items = [xlo[c, k, rows, :].astype(F32) for k in range(RAD)]
            items += [movie[k, c, rows, :].astype(F32) for k in range(cx)]
            items += [xhi[c, k, rows, :].astype(F32) for k in range(RAD)]
            for x in range(cx):
                v = blur9(items, x)
                yb[x, rows, :] = v
                xsend[c, x, rows, :] = v.astype(BF16)
            return c2

        lax.fori_loop(0, cz // ZT, tile, 0)

        @pl.when(jnp.logical_and(i % 2 == 0, has_yl))
        def _():
            y_down(i // 2).start()

        @pl.when(jnp.logical_and(i % 2 == 1, has_yh))
        def _():
            y_up(RAD - 1 - i // 2).start()

        lanes = lax.broadcasted_iota(jnp.int32, (cx * cy, fr), 0)
        for x in range(0, cx, 2):
            parts = [split(yb[x + k]) for k in range(2)]
            hi = jnp.concatenate([p[0] for p in parts], axis=1)
            lo = jnp.concatenate([p[1] for p in parts], axis=1)
            z_pair([hi, hi, lo], band[...], c + RAD, x)
            for k in range(2):
                one = jnp.where(lanes == (x + k) * cy + c, 1.0, 0.0).astype(BF16)
                maskx[c, x + k] = jnp.dot(maskt[...], one, preferred_element_type=F32).astype(BF16)
        return carry

    lax.fori_loop(0, cy, x_column, 0)

    def save(c):
        return pltpu.make_async_copy(filt.at[c], filt_hbm.at[c], fsem.at[c])

    def y_column(c):
        def tile(z, carry):
            rows = pl.ds(pl.multiple_of(z * ZT, ZT), ZT)
            for x in range(cx):
                blur = blur9([zy[c + k, x, rows, :] for k in range(2 * RAD + 1)], 0)
                f = maskx[c, x, rows, :].astype(F32) * (movie[x, c, rows, :].astype(F32) - blur)
                fh, fl = split(f)
                filt[c, x, rows, 0:fr] = fh
                filt[c, x, rows, fr:2 * fr] = fl
            return carry
        lax.fori_loop(0, cz // ZT, tile, 0)
        save(c).start()
        both = filt[c].reshape(cx * cz, 2 * fr)
        gacc[...] += lax.dot_general(
            both[:, 0:fr], both, (((0,), (0,)), ((), ())), preferred_element_type=F32)

    def y_step(j, carry):
        @pl.when(has_yl)
        def _():
            y_up(RAD - 1 - j).wait_recv()

        @pl.when(has_yh)
        def _():
            y_down(j).wait_recv()
        halo_column(ylo, RAD - 1 - j, RAD - 1 - j)
        halo_column(yhi, j, cy + RAD + j)

        def two(s, c2):
            y_column(jnp.where(s == 0, RAD - 1 - j, cy - RAD + j))
            return c2
        lax.fori_loop(0, 2, two, 0)
        return carry

    lax.fori_loop(0, RAD, y_step, 0)

    g = gacc[:, 0:fr] + gacc[:, fr:2 * fr] + jnp.transpose(gacc[:, fr:2 * fr])
    r = fr // ny
    for p in range(ny):
        gpart[p] = g[p * r:(p + 1) * r]

    def scatter(d):
        to = lax.rem(gy + d, ny)
        return pltpu.make_async_remote_copy(
            src_ref=gpart.at[to], dst_ref=rsbuf.at[d], send_sem=s1.at[d], recv_sem=r1.at[d],
            device_id=(gx, to), device_id_type=MESH)

    def across(d):
        return pltpu.make_async_remote_copy(
            src_ref=xbuf.at[gx], dst_ref=xbuf.at[gx], send_sem=s2.at[d], recv_sem=r2.at[d],
            device_id=(lax.rem(gx + d, nx), gy), device_id_type=MESH)

    def gather(d):
        return pltpu.make_async_remote_copy(
            src_ref=gfull.at[gy], dst_ref=gfull.at[gy], send_sem=s3.at[d], recv_sem=r3.at[d],
            device_id=(gx, lax.rem(gy + d, ny)), device_id_type=MESH)

    def each(n, f):
        def body(d, c):
            f(d)
            return c
        lax.fori_loop(1, n, body, 0)

    each(ny, lambda d: scatter(d).start())
    each(ny, lambda d: scatter(d).wait_recv())
    total = gpart[gy]
    for d in range(1, ny):
        total = total + rsbuf[d]
    xbuf[gx] = total
    each(nx, lambda d: across(d).start())
    each(nx, lambda d: across(d).wait_recv())
    total = xbuf[0]
    for d in range(1, nx):
        total = total + xbuf[d]
    gfull[gy] = total
    each(ny, lambda d: gather(d).start())
    each(ny, lambda d: gather(d).wait_recv())
    gram_out[...] = gfull[...]

    each(ny, lambda d: scatter(d).wait_send())
    each(nx, lambda d: across(d).wait_send())
    each(ny, lambda d: gather(d).wait_send())

    def drain_x(c, carry):
        @pl.when(has_xh)
        def _():
            x_up(c).wait_send()

        @pl.when(has_xl)
        def _():
            x_down(c).wait_send()
        return carry

    def drain_y(j, carry):
        @pl.when(has_yh)
        def _():
            y_up(j).wait_send()

        @pl.when(has_yl)
        def _():
            y_down(j).wait_send()
        return carry

    def drain_f(c, carry):
        save(c).wait()
        return carry

    lax.fori_loop(0, cy, drain_f, 0)
    lax.fori_loop(0, cy, drain_x, 0)
    lax.fori_loop(0, RAD, drain_y, 0)


BLK = 8


def pieces(v):
    hi = v.astype(BF16)
    rest = v - hi.astype(F32)
    mid = rest.astype(BF16)
    return hi, mid, (rest - mid.astype(F32)).astype(BF16)


def outer(u, v):
    uh, um, ul = pieces(u)
    vh, vm, vl = pieces(v)
    left = jnp.concatenate([uh, uh, um, uh, ul, um], axis=0)
    right = jnp.concatenate([vh, vm, vh, vl, vh, vm], axis=0)
    return lax.dot_general(left, right, (((0,), (0,)), ((), ())), preferred_element_type=F32)


def stack(rows, sub):
    full = rows[0]
    for i in range(1, BLK):
        full = jnp.where(sub == i, rows[i], full)
    return full


def sweep(a, dbuf, zbuf):
    n = a.shape[0]
    cols = lax.broadcasted_iota(jnp.int32, (n, n), 1)
    lane = lax.broadcasted_iota(jnp.int32, (BLK, n), 1)
    sub = lax.broadcasted_iota(jnp.int32, (BLK, n), 0)
    panel = a[0:BLK, :]
    for start in range(0, n, BLK):
        after = start + BLK
        inside = (lane >= start) & (lane < after)
        u = jnp.where(inside, 0.0, panel)
        zbuf[start // BLK % 2] = jnp.where(lane == start + sub, -1.0, u)
        slot = start // BLK % 2
        for j in range(BLK):
            dbuf[slot, j] = jnp.broadcast_to(panel[:, start + j:start + j + 1], (BLK, n))
        if after < n:
            for j in range(BLK):
                dbuf[slot, BLK + j] = jnp.broadcast_to(panel[:, after + j:after + j + 1], (BLK, n))

        def entry(i, j):
            return jnp.broadcast_to(dbuf[slot, j, i:i + 1, :], (BLK, n))

        d = {(i, j): entry(i, j) for j in range(BLK) for i in range(j + 1)}
        z = [jnp.broadcast_to(zbuf[slot, i:i + 1, :], (BLK, n)) for i in range(BLK)]
        inverses, multipliers = {}, {}
        for s in range(0, BLK, 2):
            p, q, r = d[s, s], d[s, s + 1], d[s + 1, s + 1]
            inv = 1.0 / (p * r - q * q)
            ip, iq, ir = r * inv, -(q * inv), p * inv
            inverses[s] = (ip, iq, ir)
            for i in range(s + 2, BLK):
                m0 = d[s, i] * ip + d[s + 1, i] * iq
                m1 = d[s, i] * iq + d[s + 1, i] * ir
                multipliers[s, i] = (m0, m1)
                for j in range(i, BLK):
                    d[i, j] = d[i, j] - (m0 * d[s, j] + m1 * d[s + 1, j])
                z[i] = z[i] - (m0 * z[s] + m1 * z[s + 1])
        for s in range(BLK - 2, -1, -2):
            ip, iq, ir = inverses[s]
            w0, w1 = ip * z[s] + iq * z[s + 1], iq * z[s] + ir * z[s + 1]
            for i in range(BLK - 1, s + 1, -1):
                m0, m1 = multipliers[s, i]
                w0, w1 = w0 - m0 * z[i], w1 - m1 * z[i]
            z[s], z[s + 1] = w0, w1
        if after < n:
            rows = []
            for i in range(BLK):
                terms = [entry(s, BLK + i) * z[s] for s in range(BLK)]
                while len(terms) > 1:
                    terms = [terms[k] + terms[k + 1] for k in range(0, len(terms), 2)]
                rows.append(terms[0])
            panel = jnp.where(inside, 0.0, a[after:after + BLK, :]) - stack(rows, sub)
        full = stack(z, sub)
        a[...] = jnp.where((cols >= start) & (cols < after), 0.0, a[...]) - outer(u, full)
        a[start:after, :] = full


def fit_kernel(gram, filt_hbm, out_hbm, prop, a, m, dbuf, zbuf, filt, out, isem, osem):
    fr = gram.shape[0]
    load = pltpu.make_async_copy(filt_hbm, filt, isem.at[0])
    load.start()

    g = gram[...]
    row = lax.broadcasted_iota(jnp.int32, (fr, fr), 0)
    col = lax.broadcasted_iota(jnp.int32, (fr, fr), 1)
    diag = jnp.where((row == col) & (row < fr - 1), g, 0.0)
    lam = 0.5 * jnp.sum(diag) / (fr - 1)
    scaled = g / lam
    last = (row == fr - 1) | (col == fr - 1)
    a[...] = jnp.where(last, 0.0, scaled) + jnp.where(row == col, 1.0, 0.0)
    sweep(a, dbuf, zbuf)
    x = -jnp.dot(a[...], jnp.where(row == fr - 1, 0.0, scaled),
                 precision=lax.Precision.HIGHEST, preferred_element_type=F32)
    prop[...] = x[0:fr - 1, 1:fr]
    adv = jnp.where(col == 0, jnp.where(row == 0, 1.0, 0.0), x)
    mh, ml = split(adv)
    m[0:fr, 0:fr] = mh
    m[0:fr, fr:2 * fr] = ml
    m[fr:2 * fr, 0:fr] = mh
    m[fr:2 * fr, fr:2 * fr] = jnp.zeros((fr, fr), BF16)

    load.wait()

    def save(i):
        return pltpu.make_async_copy(out.at[i], out_hbm.at[i], osem.at[i])

    def layer(i, c):
        rows = filt[:, i].reshape(-1, 2 * fr)
        v = jnp.dot(rows, m[...], preferred_element_type=F32)
        out[i] = (v[:, 0:fr] + v[:, fr:2 * fr]).astype(BF16).reshape(out.shape[1:])
        save(i).start()
        return c

    def drain(i, c):
        save(i).wait()
        return c

    lax.fori_loop(0, out.shape[0], layer, 0)
    lax.fori_loop(0, out.shape[0], drain, 0)


def on_device(nx, ny, movie, brain_mask):
    cx, cy, cz, fr = movie.shape
    r = fr // ny
    vmem = pl.BlockSpec(memory_space=pltpu.VMEM)
    hbm = pl.BlockSpec(memory_space=pltpu.HBM)
    dma = pltpu.SemaphoreType.DMA
    filt, gram = pl.pallas_call(
        functools.partial(filter_kernel, nx, ny),
        out_shape=(
            jax.ShapeDtypeStruct((cy, cx, cz, 2 * fr), BF16),
            jax.ShapeDtypeStruct((ny, r, fr), F32),
        ),
        in_specs=[hbm, hbm],
        out_specs=(hbm, vmem),
        scratch_shapes=[
            pltpu.VMEM((cx, cy, cz, fr), BF16),
            pltpu.VMEM((cx, cy, cz), jnp.int32),
            dma((2,)),
            pltpu.VMEM((cy, cx, cz, 2 * fr), BF16),
            dma((cy,)),
            pltpu.VMEM((cy, RAD, cz, fr), BF16),
            pltpu.VMEM((cy, RAD, cz, fr), BF16),
            pltpu.VMEM((cy, cx, cz, fr), BF16),
            pltpu.VMEM((RAD, cx, cz, fr), BF16),
            pltpu.VMEM((RAD, cx, cz, fr), BF16),
            pltpu.VMEM((cy + 2 * RAD, cx, cz, fr), F32),
            pltpu.VMEM((cx, cz, fr), F32),
            pltpu.VMEM((cy, cx, cz, fr), BF16),
            pltpu.VMEM((cz, 3 * cz), BF16),
            pltpu.VMEM((cz, cx * cy), BF16),
            pltpu.VMEM((fr, 2 * fr), F32),
            pltpu.VMEM((ny, r, fr), F32),
            pltpu.VMEM((ny, r, fr), F32),
            pltpu.VMEM((nx, r, fr), F32),
            pltpu.VMEM((ny, r, fr), F32),
            dma((cy,)), dma((cy,)), dma((cy,)), dma((cy,)),
            dma((RAD,)), dma((RAD,)), dma((RAD,)), dma((RAD,)),
            dma((ny,)), dma((ny,)), dma((nx,)), dma((nx,)), dma((ny,)), dma((ny,)),
        ],
        compiler_params=pltpu.CompilerParams(
            collective_id=0, has_side_effects=True, vmem_limit_bytes=60 * 1024 * 1024),
    )(movie, brain_mask)
    gram = gram.reshape(fr, fr)
    fitted, propagator = pl.pallas_call(
        fit_kernel,
        out_shape=(
            jax.ShapeDtypeStruct((cx, cy, cz, fr), BF16),
            jax.ShapeDtypeStruct((fr - 1, fr - 1), F32),
        ),
        in_specs=[vmem, hbm],
        out_specs=(hbm, vmem),
        scratch_shapes=[
            pltpu.VMEM((fr, fr), F32),
            pltpu.VMEM((2 * fr, 2 * fr), BF16),
            pltpu.VMEM((2, 2 * BLK, BLK, fr), F32),
            pltpu.VMEM((2, BLK, fr), F32),
            pltpu.VMEM((cy, cx, cz, 2 * fr), BF16),
            pltpu.VMEM((cx, cy, cz, fr), BF16),
            dma((1,)),
            dma((cx,)),
        ],
        compiler_params=pltpu.CompilerParams(vmem_limit_bytes=60 * 1024 * 1024),
    )(gram, filt)
    return fitted, propagator


def solution(mesh):
    nx, ny = mesh.shape["gx"], mesh.shape["gy"]
    return jax.shard_map(
        functools.partial(on_device, nx, ny),
        mesh=mesh,
        in_specs=(P("gx", "gy", None, None), P("gx", "gy", None)),
        out_specs=(P("gx", "gy", None, None), P()),
        check_vma=False,
    )
```

```python
import functools

import numpy as np
import jax
import jax.numpy as jnp
from jax import lax
from jax.experimental import pallas as pl
from jax.experimental.pallas import tpu as pltpu
from jax.sharding import PartitionSpec as P

RAD = 4
AHEAD = 5
MESH = pl.DeviceIdType.MESH
F32 = jnp.float32
BF16 = jnp.bfloat16


def weights():
    k = np.arange(-RAD, RAD + 1).astype(np.float32)
    sigma = RAD / 2.0
    raw = np.exp(-k * k / np.float32(2.0 * sigma * sigma)).astype(np.float32)
    w = raw / raw.sum(dtype=np.float32)
    return [float(w[RAD + j]) for j in range(RAD + 1)]


W = weights()


def blur9(items, at):
    total = W[0] * items[at + RAD]
    for k in range(1, RAD + 1):
        total = total + W[k] * (items[at + RAD - k] + items[at + RAD + k])
    return total


def split(v):
    hi = v.astype(BF16)
    return hi, (v - hi.astype(F32)).astype(BF16)


def filter_kernel(
    nx, ny,
    movie_hbm, mask_hbm, filt_hbm, gram_out,
    movie, mask, local, filt, fsem, xlo, xhi, xsend, ylo, yhi, zy, yb, maskx, band, maskt, gacc, gpart, rsbuf, xbuf, gfull,
    xsl, xsh, xrl, xrh, ysl, ysh, yrl, yrh, s1, r1, s2, r2, s3, r3,
):
    cx, cy, cz, fr = movie.shape
    gx, gy = lax.axis_index("gx"), lax.axis_index("gy")
    load_movie = pltpu.make_async_copy(movie_hbm, movie, local.at[0])
    load_mask = pltpu.make_async_copy(mask_hbm, mask, local.at[1])
    load_movie.start()
    load_mask.start()
    barrier = pltpu.get_barrier_semaphore()

    def hello_y(d, c):
        pl.semaphore_signal(barrier, inc=1, device_id=(gx, lax.rem(gy + d, ny)), device_id_type=MESH)
        return c

    def hello_x(d, c):
        pl.semaphore_signal(barrier, inc=1, device_id=(lax.rem(gx + d, nx), gy), device_id_type=MESH)
        return c

    lax.fori_loop(1, ny, hello_y, 0)
    lax.fori_loop(1, nx, hello_x, 0)
    pl.semaphore_wait(barrier, ny - 1 + nx - 1)

    has_yl, has_yh = gy > 0, gy < ny - 1
    has_xl, has_xh = gx > 0, gx < nx - 1

    def order(i):
        return jnp.where(i % 2 == 0, i // 2, cy - 1 - i // 2)

    def x_up(c):
        return pltpu.make_async_remote_copy(
            src_ref=movie_hbm.at[pl.ds(cx - RAD, RAD), c], dst_ref=xlo.at[c],
            send_sem=xsl.at[c], recv_sem=xrl.at[c],
            device_id=(gx + 1, gy), device_id_type=MESH)

    def x_down(c):
        return pltpu.make_async_remote_copy(
            src_ref=movie_hbm.at[pl.ds(0, RAD), c], dst_ref=xhi.at[c],
            send_sem=xsh.at[c], recv_sem=xrh.at[c],
            device_id=(gx - 1, gy), device_id_type=MESH)

    def y_up(j):
        return pltpu.make_async_remote_copy(
            src_ref=xsend.at[cy - RAD + j], dst_ref=ylo.at[j],
            send_sem=ysl.at[j], recv_sem=yrl.at[j],
            device_id=(gx, gy + 1), device_id_type=MESH)

    def y_down(j):
        return pltpu.make_async_remote_copy(
            src_ref=xsend.at[j], dst_ref=yhi.at[j],
            send_sem=ysh.at[j], recv_sem=yrh.at[j],
            device_id=(gx, gy - 1), device_id_type=MESH)

    def start_x(i, carry):
        c = order(i)

        @pl.when(has_xh)
        def _():
            x_up(c).start()

        @pl.when(has_xl)
        def _():
            x_down(c).start()
        return carry

    lax.fori_loop(0, AHEAD, start_x, 0)

    @pl.when(jnp.logical_not(has_yl))
    def _():
        ylo[...] = jnp.zeros_like(ylo)

    @pl.when(jnp.logical_not(has_yh))
    def _():
        yhi[...] = jnp.zeros_like(yhi)

    @pl.when(jnp.logical_not(has_xl))
    def _():
        xlo[...] = jnp.zeros_like(xlo)

    @pl.when(jnp.logical_not(has_xh))
    def _():
        xhi[...] = jnp.zeros_like(xhi)

    dist = jnp.abs(lax.broadcasted_iota(jnp.int32, (cz, cz), 0) - lax.broadcasted_iota(jnp.int32, (cz, cz), 1))
    t = jnp.zeros((cz, cz), F32)
    for k in range(RAD + 1):
        t = jnp.where(dist == k, W[k], t)
    th, tl = split(t)
    band[:, 0:cz] = th
    band[:, cz:2 * cz] = tl
    band[:, 2 * cz:3 * cz] = th
    load_mask.wait()
    maskt[...] = jnp.transpose(mask[...].astype(F32).reshape(cx * cy, cz)).astype(BF16)
    gacc[...] = jnp.zeros_like(gacc)

    load_movie.wait()
    ZT = 16

    def z_pair(pieces, lhs, to, y):
        v = jnp.dot(lhs, jnp.concatenate(pieces, axis=0), preferred_element_type=F32)
        zy[to, y] = v[:, 0:fr]
        zy[to, y + 1] = v[:, fr:2 * fr]

    def halo_column(src, j, to):
        for x in range(0, cx, 2):
            h = jnp.concatenate([src[j, x], src[j, x + 1]], axis=1)
            z_pair([h, h], band[:, 0:2 * cz], to, x)

    def x_column(i, carry):
        c = order(i)

        @pl.when(has_xl)
        def _():
            x_up(c).wait_recv()

        @pl.when(has_xh)
        def _():
            x_down(c).wait_recv()

        @pl.when(i + AHEAD < cy)
        def _():
            start_x(i + AHEAD, 0)

        def tile(z, c2):
            rows = pl.ds(pl.multiple_of(z * ZT, ZT), ZT)
            items = [xlo[c, k, rows, :].astype(F32) for k in range(RAD)]
            items += [movie[k, c, rows, :].astype(F32) for k in range(cx)]
            items += [xhi[c, k, rows, :].astype(F32) for k in range(RAD)]
            for x in range(cx):
                v = blur9(items, x)
                yb[x, rows, :] = v
                xsend[c, x, rows, :] = v.astype(BF16)
            return c2

        lax.fori_loop(0, cz // ZT, tile, 0)

        @pl.when(jnp.logical_and(i % 2 == 0, has_yl))
        def _():
            y_down(i // 2).start()

        @pl.when(jnp.logical_and(i % 2 == 1, has_yh))
        def _():
            y_up(RAD - 1 - i // 2).start()

        lanes = lax.broadcasted_iota(jnp.int32, (cx * cy, fr), 0)
        for x in range(0, cx, 2):
            parts = [split(yb[x + k]) for k in range(2)]
            hi = jnp.concatenate([p[0] for p in parts], axis=1)
            lo = jnp.concatenate([p[1] for p in parts], axis=1)
            z_pair([hi, hi, lo], band[...], c + RAD, x)
            for k in range(2):
                one = jnp.where(lanes == (x + k) * cy + c, 1.0, 0.0).astype(BF16)
                maskx[c, x + k] = jnp.dot(maskt[...], one, preferred_element_type=F32).astype(BF16)
        return carry

    lax.fori_loop(0, cy, x_column, 0)

    def save(c):
        return pltpu.make_async_copy(filt.at[c], filt_hbm.at[c], fsem.at[c])

    def y_column(c):
        def tile(z, carry):
            rows = pl.ds(pl.multiple_of(z * ZT, ZT), ZT)
            for x in range(cx):
                blur = blur9([zy[c + k, x, rows, :] for k in range(2 * RAD + 1)], 0)
                f = maskx[c, x, rows, :].astype(F32) * (movie[x, c, rows, :].astype(F32) - blur)
                fh, fl = split(f)
                filt[c, x, rows, 0:fr] = fh
                filt[c, x, rows, fr:2 * fr] = fl
            return carry
        lax.fori_loop(0, cz // ZT, tile, 0)
        save(c).start()
        both = filt[c].reshape(cx * cz, 2 * fr)
        gacc[...] += lax.dot_general(
            both[:, 0:fr], both, (((0,), (0,)), ((), ())), preferred_element_type=F32)

    def y_step(j, carry):
        @pl.when(has_yl)
        def _():
            y_up(RAD - 1 - j).wait_recv()

        @pl.when(has_yh)
        def _():
            y_down(j).wait_recv()
        halo_column(ylo, RAD - 1 - j, RAD - 1 - j)
        halo_column(yhi, j, cy + RAD + j)

        def two(s, c2):
            y_column(jnp.where(s == 0, RAD - 1 - j, cy - RAD + j))
            return c2
        lax.fori_loop(0, 2, two, 0)
        return carry

    lax.fori_loop(0, RAD, y_step, 0)

    g = gacc[:, 0:fr] + gacc[:, fr:2 * fr] + jnp.transpose(gacc[:, fr:2 * fr])
    r = fr // ny
    for p in range(ny):
        gpart[p] = g[p * r:(p + 1) * r]

    def scatter(d):
        to = lax.rem(gy + d, ny)
        return pltpu.make_async_remote_copy(
            src_ref=gpart.at[to], dst_ref=rsbuf.at[d], send_sem=s1.at[d], recv_sem=r1.at[d],
            device_id=(gx, to), device_id_type=MESH)

    def across(d):
        return pltpu.make_async_remote_copy(
            src_ref=xbuf.at[gx], dst_ref=xbuf.at[gx], send_sem=s2.at[d], recv_sem=r2.at[d],
            device_id=(lax.rem(gx + d, nx), gy), device_id_type=MESH)

    def gather(d):
        return pltpu.make_async_remote_copy(
            src_ref=gfull.at[gy], dst_ref=gfull.at[gy], send_sem=s3.at[d], recv_sem=r3.at[d],
            device_id=(gx, lax.rem(gy + d, ny)), device_id_type=MESH)

    def each(n, f):
        def body(d, c):
            f(d)
            return c
        lax.fori_loop(1, n, body, 0)

    each(ny, lambda d: scatter(d).start())
    each(ny, lambda d: scatter(d).wait_recv())
    total = gpart[gy]
    for d in range(1, ny):
        total = total + rsbuf[d]
    xbuf[gx] = total
    each(nx, lambda d: across(d).start())
    each(nx, lambda d: across(d).wait_recv())
    total = xbuf[0]
    for d in range(1, nx):
        total = total + xbuf[d]
    gfull[gy] = total
    each(ny, lambda d: gather(d).start())
    each(ny, lambda d: gather(d).wait_recv())
    gram_out[...] = gfull[...]

    each(ny, lambda d: scatter(d).wait_send())
    each(nx, lambda d: across(d).wait_send())
    each(ny, lambda d: gather(d).wait_send())

    def drain_x(c, carry):
        @pl.when(has_xh)
        def _():
            x_up(c).wait_send()

        @pl.when(has_xl)
        def _():
            x_down(c).wait_send()
        return carry

    def drain_y(j, carry):
        @pl.when(has_yh)
        def _():
            y_up(j).wait_send()

        @pl.when(has_yl)
        def _():
            y_down(j).wait_send()
        return carry

    def drain_f(c, carry):
        save(c).wait()
        return carry

    lax.fori_loop(0, cy, drain_f, 0)
    lax.fori_loop(0, cy, drain_x, 0)
    lax.fori_loop(0, RAD, drain_y, 0)


BLK = 8


def pieces(v):
    hi = v.astype(BF16)
    rest = v - hi.astype(F32)
    mid = rest.astype(BF16)
    return hi, mid, (rest - mid.astype(F32)).astype(BF16)


def outer(u, v):
    uh, um, ul = pieces(u)
    vh, vm, vl = pieces(v)
    left = jnp.concatenate([uh, uh, um, uh, ul, um], axis=0)
    right = jnp.concatenate([vh, vm, vh, vl, vh, vm], axis=0)
    return lax.dot_general(left, right, (((0,), (0,)), ((), ())), preferred_element_type=F32)


def stack(rows, sub):
    full = rows[0]
    for i in range(1, BLK):
        full = jnp.where(sub == i, rows[i], full)
    return full


def sweep(a, dbuf, zbuf):
    n = a.shape[0]
    cols = lax.broadcasted_iota(jnp.int32, (n, n), 1)
    lane = lax.broadcasted_iota(jnp.int32, (BLK, n), 1)
    sub = lax.broadcasted_iota(jnp.int32, (BLK, n), 0)
    panel = a[0:BLK, :]
    for start in range(0, n, BLK):
        after = start + BLK
        inside = (lane >= start) & (lane < after)
        u = jnp.where(inside, 0.0, panel)
        zbuf[start // BLK % 2] = jnp.where(lane == start + sub, -1.0, u)
        slot = start // BLK % 2
        for j in range(BLK):
            dbuf[slot, j] = jnp.broadcast_to(panel[:, start + j:start + j + 1], (BLK, n))
        if after < n:
            for j in range(BLK):
                dbuf[slot, BLK + j] = jnp.broadcast_to(panel[:, after + j:after + j + 1], (BLK, n))

        def entry(i, j):
            return jnp.broadcast_to(dbuf[slot, j, i:i + 1, :], (BLK, n))

        d = {(i, j): entry(i, j) for j in range(BLK) for i in range(j + 1)}
        z = [jnp.broadcast_to(zbuf[slot, i:i + 1, :], (BLK, n)) for i in range(BLK)]
        inverses, multipliers = {}, {}
        for s in range(0, BLK, 2):
            p, q, r = d[s, s], d[s, s + 1], d[s + 1, s + 1]
            inv = 1.0 / (p * r - q * q)
            ip, iq, ir = r * inv, -(q * inv), p * inv
            inverses[s] = (ip, iq, ir)
            for i in range(s + 2, BLK):
                m0 = d[s, i] * ip + d[s + 1, i] * iq
                m1 = d[s, i] * iq + d[s + 1, i] * ir
                multipliers[s, i] = (m0, m1)
                for j in range(i, BLK):
                    d[i, j] = d[i, j] - (m0 * d[s, j] + m1 * d[s + 1, j])
                z[i] = z[i] - (m0 * z[s] + m1 * z[s + 1])
        for s in range(BLK - 2, -1, -2):
            ip, iq, ir = inverses[s]
            w0, w1 = ip * z[s] + iq * z[s + 1], iq * z[s] + ir * z[s + 1]
            for i in range(BLK - 1, s + 1, -1):
                m0, m1 = multipliers[s, i]
                w0, w1 = w0 - m0 * z[i], w1 - m1 * z[i]
            z[s], z[s + 1] = w0, w1
        if after < n:
            rows = []
            for i in range(BLK):
                terms = [entry(s, BLK + i) * z[s] for s in range(BLK)]
                while len(terms) > 1:
                    terms = [terms[k] + terms[k + 1] for k in range(0, len(terms), 2)]
                rows.append(terms[0])
            panel = jnp.where(inside, 0.0, a[after:after + BLK, :]) - stack(rows, sub)
        full = stack(z, sub)
        a[...] = jnp.where((cols >= start) & (cols < after), 0.0, a[...]) - outer(u, full)
        a[start:after, :] = full


def fit_kernel(gram, filt_hbm, out_hbm, prop, a, m, dbuf, zbuf, filt, out, isem, osem):
    fr = gram.shape[0]
    load = pltpu.make_async_copy(filt_hbm, filt, isem.at[0])
    load.start()

    g = gram[...]
    row = lax.broadcasted_iota(jnp.int32, (fr, fr), 0)
    col = lax.broadcasted_iota(jnp.int32, (fr, fr), 1)
    diag = jnp.where((row == col) & (row < fr - 1), g, 0.0)
    lam = 0.5 * jnp.sum(diag) / (fr - 1)
    scaled = g / lam
    last = (row == fr - 1) | (col == fr - 1)
    a[...] = jnp.where(last, 0.0, scaled) + jnp.where(row == col, 1.0, 0.0)
    sweep(a, dbuf, zbuf)
    x = -jnp.dot(a[...], jnp.where(row == fr - 1, 0.0, scaled),
                 precision=lax.Precision.HIGHEST, preferred_element_type=F32)
    prop[...] = x[0:fr - 1, 1:fr]
    adv = jnp.where(col == 0, jnp.where(row == 0, 1.0, 0.0), x)
    mh, ml = split(adv)
    m[0:fr, 0:fr] = mh
    m[0:fr, fr:2 * fr] = ml
    m[fr:2 * fr, 0:fr] = mh
    m[fr:2 * fr, fr:2 * fr] = jnp.zeros((fr, fr), BF16)

    load.wait()

    def save(i):
        return pltpu.make_async_copy(out.at[i], out_hbm.at[i], osem.at[i])

    def layer(i, c):
        rows = filt[:, i].reshape(-1, 2 * fr)
        v = jnp.dot(rows, m[...], preferred_element_type=F32)
        out[i] = (v[:, 0:fr] + v[:, fr:2 * fr]).astype(BF16).reshape(out.shape[1:])
        save(i).start()
        return c

    def drain(i, c):
        save(i).wait()
        return c

    lax.fori_loop(0, out.shape[0], layer, 0)
    lax.fori_loop(0, out.shape[0], drain, 0)


def on_device(nx, ny, movie, brain_mask):
    cx, cy, cz, fr = movie.shape
    r = fr // ny
    vmem = pl.BlockSpec(memory_space=pltpu.VMEM)
    hbm = pl.BlockSpec(memory_space=pltpu.HBM)
    dma = pltpu.SemaphoreType.DMA
    filt, gram = pl.pallas_call(
        functools.partial(filter_kernel, nx, ny),
        out_shape=(
            jax.ShapeDtypeStruct((cy, cx, cz, 2 * fr), BF16),
            jax.ShapeDtypeStruct((ny, r, fr), F32),
        ),
        in_specs=[hbm, hbm],
        out_specs=(hbm, vmem),
        scratch_shapes=[
            pltpu.VMEM((cx, cy, cz, fr), BF16),
            pltpu.VMEM((cx, cy, cz), jnp.int32),
            dma((2,)),
            pltpu.VMEM((cy, cx, cz, 2 * fr), BF16),
            dma((cy,)),
            pltpu.VMEM((cy, RAD, cz, fr), BF16),
            pltpu.VMEM((cy, RAD, cz, fr), BF16),
            pltpu.VMEM((cy, cx, cz, fr), BF16),
            pltpu.VMEM((RAD, cx, cz, fr), BF16),
            pltpu.VMEM((RAD, cx, cz, fr), BF16),
            pltpu.VMEM((cy + 2 * RAD, cx, cz, fr), F32),
            pltpu.VMEM((cx, cz, fr), F32),
            pltpu.VMEM((cy, cx, cz, fr), BF16),
            pltpu.VMEM((cz, 3 * cz), BF16),
            pltpu.VMEM((cz, cx * cy), BF16),
            pltpu.VMEM((fr, 2 * fr), F32),
            pltpu.VMEM((ny, r, fr), F32),
            pltpu.VMEM((ny, r, fr), F32),
            pltpu.VMEM((nx, r, fr), F32),
            pltpu.VMEM((ny, r, fr), F32),
            dma((cy,)), dma((cy,)), dma((cy,)), dma((cy,)),
            dma((RAD,)), dma((RAD,)), dma((RAD,)), dma((RAD,)),
            dma((ny,)), dma((ny,)), dma((nx,)), dma((nx,)), dma((ny,)), dma((ny,)),
        ],
        compiler_params=pltpu.CompilerParams(
            collective_id=0, has_side_effects=True, vmem_limit_bytes=60 * 1024 * 1024),
    )(movie, brain_mask)
    gram = gram.reshape(fr, fr)
    fitted, propagator = pl.pallas_call(
        fit_kernel,
        out_shape=(
            jax.ShapeDtypeStruct((cx, cy, cz, fr), BF16),
            jax.ShapeDtypeStruct((fr - 1, fr - 1), F32),
        ),
        in_specs=[vmem, hbm],
        out_specs=(hbm, vmem),
        scratch_shapes=[
            pltpu.VMEM((fr, fr), F32),
            pltpu.VMEM((2 * fr, 2 * fr), BF16),
            pltpu.VMEM((2, 2 * BLK, BLK, fr), F32),
            pltpu.VMEM((2, BLK, fr), F32),
            pltpu.VMEM((cy, cx, cz, 2 * fr), BF16),
            pltpu.VMEM((cx, cy, cz, fr), BF16),
            dma((1,)),
            dma((cx,)),
        ],
        compiler_params=pltpu.CompilerParams(vmem_limit_bytes=60 * 1024 * 1024),
    )(gram, filt)
    return fitted, propagator


def solution(mesh):
    nx, ny = mesh.shape["gx"], mesh.shape["gy"]
    return jax.shard_map(
        functools.partial(on_device, nx, ny),
        mesh=mesh,
        in_specs=(P("gx", "gy", None, None), P("gx", "gy", None)),
        out_specs=(P("gx", "gy", None, None), P()),
        check_vma=False,
    )
```
